128 devices in a mesh: seg: 8 (over z, core), sec: 16 (over x, y).
Axes of the slice: x: 4, y: 4, z: 4, core: 2. Of those that a mesh axis runs over, the one named last changes fastest.
Arguments:
- wave_first: float32 [8, 128, 128, 128], P('seg', 'sec')
- wave_second: float32 [8, 128, 128, 128], P('seg', 'sec')
- onsite_first: float32 [8, 128, 128, 128], P('seg', 'sec'), may hold values from 0.5 to 4
- onsite_second: float32 [8, 128, 128, 128], P('seg', 'sec'), may hold values from 0.5 to 4
- left_first: bfloat16 [8, 128, 16, 128, 128], P('seg', 'sec'), may hold values from -0.5 to 0.5
- right_first: bfloat16 [8, 128, 16, 128, 128], P('seg', 'sec'), may hold values from -0.125 to 0.125
- left_base: bfloat16 [8, 128, 16, 128, 128], P('seg', 'sec'), may hold values from -0.5 to 0.5
- right_second: bfloat16 [8, 128, 16, 128, 128], P('seg', 'sec'), may hold values from -0.125 to 0.125
- sources: int32 [128, 16], P('sec'), may hold values from 0 to 127, as said below
- block_dims: int32 [128], P('sec'), may hold values from 8 to 128, as said below
Outputs:
- result_first: float32 [8, 128, 128, 128], P('seg', 'sec')
- result_second: float32 [8, 128, 128, 128], P('seg', 'sec')
The draws below stay inside these ranges and needn't reach their ends.
Inputs may be any that keep to these rules, and one draw needn't show every extreme that they name: `sources`: each entry names a block whose index differs from its row's block by at most 8, and that difference is reached. `block_dims`: a multiple of 8.
All inputs are finite; a program needn't handle non-finite values.
Results may differ from the reference program's by a relative error of at most 0.015.
Values may be sent and summed in bfloat16 or wider, within the bound.
A program may use at most 128 MiB of HBM per device.

```python
import math
import jax
import jax.numpy as jnp
from jax import lax

P_SIZE = 128
K = 16
STEPS = 3
BLK_DEV = 8
NBLK = 128
SEGS = 8


def wave_field(key):
    keys = jax.random.split(key, 3)
    shape = (SEGS, NBLK, P_SIZE, P_SIZE)
    base = jax.random.normal(keys[0], shape, jnp.float32)
    row_scale = jnp.exp(jax.random.uniform(keys[1], (SEGS, NBLK, P_SIZE, 1), jnp.float32, 0.0, math.log(10.0)))
    col_scale = jnp.exp(jax.random.uniform(keys[2], (SEGS, NBLK, 1, P_SIZE), jnp.float32, 0.0, math.log(10.0)))
    rising = 1.0 + 2.0 * jnp.arange(NBLK, dtype=jnp.float32) / max(NBLK - 1, 1)
    return 0.1 * base * row_scale * col_scale * rising[None, :, None, None]


def draw_wave_first(key, part):
    return wave_field(jax.random.fold_in(key, 11))


def draw_wave_second(key, part):
    return wave_field(jax.random.fold_in(key, 23))


def draw_sources(key, part):
    offsets = jax.random.randint(jax.random.fold_in(key, 37), (NBLK, K), -BLK_DEV, BLK_DEV + 1)
    column = jnp.arange(K, dtype=jnp.int32)[None, :]
    offsets = jnp.where(column == 0, BLK_DEV, jnp.where(column == 1, -BLK_DEV, offsets))
    target = jnp.arange(NBLK, dtype=jnp.int32)[:, None] + offsets
    return jnp.clip(target, 0, NBLK - 1).astype(jnp.int32)


def draw_block_dims(key, part):
    sizes = jax.random.randint(jax.random.fold_in(key, 41), (NBLK,), 1, P_SIZE // 8 + 1) * 8
    first = jnp.arange(NBLK, dtype=jnp.int32) == 0
    return jnp.where(first, P_SIZE, sizes).astype(jnp.int32)


def steps_of(stream_key, extent, pieces, low, top_value):
    gain = 1.0
    for dim, blocks in pieces:
        heights = jax.random.uniform(jax.random.fold_in(jax.random.fold_in(stream_key, 6), dim), (blocks,), jnp.float32, low / len(pieces), top_value / len(pieces))
        gain = gain * jnp.repeat(jnp.exp(heights), extent[dim] // blocks).reshape((-1,) + (1,) * (len(extent) - 1 - dim))
    return gain


def bell_draw(rng, extent, scale, most, cuts=(), held_as=jnp.bfloat16):
    values = jax.random.normal(rng, extent, jnp.float32) * scale
    if len(cuts) > 0:
        values = steps_of(rng, extent, cuts, -0.22, 0.18) * values
    return jnp.clip(values, min=-most, max=most).astype(held_as)


def setup_inputs(seed: int = 0) -> dict:
    arg_keys = jax.random.split(jax.random.key(seed), 11)
    return {
        "wave_first": draw_wave_first(jax.random.fold_in(arg_keys[10], 71), 0),
        "wave_second": draw_wave_second(jax.random.fold_in(arg_keys[10], 71), 0),
        "onsite_first": jnp.clip(jnp.exp(math.log(4.0) - 2.0794415 * jax.random.uniform(arg_keys[2], (SEGS, NBLK, P_SIZE, P_SIZE), jnp.float32) ** steps_of(arg_keys[2], (SEGS, NBLK, P_SIZE, P_SIZE), ((0, 8), (1, 16)), -0.2, 0.2)), 0.5, 4.0),
        "onsite_second": jnp.clip(jnp.exp(math.log(4.0) - 2.0794415 * jax.random.uniform(arg_keys[3], (SEGS, NBLK, P_SIZE, P_SIZE), jnp.float32) ** steps_of(arg_keys[3], (SEGS, NBLK, P_SIZE, P_SIZE), ((0, 8), (1, 16)), -0.2, 0.2)), 0.5, 4.0),
        "left_first": bell_draw(arg_keys[4], (SEGS, NBLK, K, P_SIZE, P_SIZE), P_SIZE ** -0.5, 0.5, ((0, 8), (1, 16))),
        "right_first": bell_draw(arg_keys[5], (SEGS, NBLK, K, P_SIZE, P_SIZE), (P_SIZE * K) ** -0.5, 0.125, ((0, 8), (1, 16))),
        "left_base": bell_draw(arg_keys[6], (SEGS, NBLK, K, P_SIZE, P_SIZE), P_SIZE ** -0.5, 0.5, ((0, 8), (1, 16))),
        "right_second": bell_draw(arg_keys[7], (SEGS, NBLK, K, P_SIZE, P_SIZE), (P_SIZE * K) ** -0.5, 0.125, ((0, 8), (1, 16))),
        "sources": draw_sources(jax.random.fold_in(arg_keys[10], 71), 0),
        "block_dims": draw_block_dims(jax.random.fold_in(arg_keys[10], 71), 0),
    }


def live_mask(block_dims):
    row_index = lax.broadcasted_iota(jnp.int32, (block_dims.shape[0], P_SIZE, P_SIZE), 1)
    col_index = lax.broadcasted_iota(jnp.int32, (block_dims.shape[0], P_SIZE, P_SIZE), 2)
    limit = block_dims[:, None, None]
    return ((row_index < limit) & (col_index < limit)).astype(jnp.float32)

def operate(vector, onsite, live, left_env, right_env, sources):
    packed = vector.astype(jnp.bfloat16)
    picked = packed[sources].astype(jnp.float32)
    left_part = jnp.einsum('bkij,bkjl->bkil', left_env.astype(jnp.float32), picked).astype(jnp.bfloat16)
    terms = jnp.einsum('bkil,bklm->bim', left_part.astype(jnp.float32), right_env.astype(jnp.float32))
    return live * (onsite * vector + terms)

def davidson(start, onsite, left_env, right_env, live, sources):
    vector = live * start
    for iteration in range(STEPS):
        image = operate(vector, onsite, live, left_env, right_env, sources)
        quotient = jnp.sum(vector * image) / jnp.sum(vector * vector)
        change = (image - quotient * vector) / (onsite + 1.0)
        moved = vector - change
        vector = moved / jnp.sqrt(jnp.sum(moved * moved) / (NBLK * P_SIZE * P_SIZE) + 1e-06)
    return vector

def build_left(pair):
    handed, base = pair
    handed_f = handed.astype(jnp.float32)
    carried = jnp.einsum('bkij,bjl->bkil', base.astype(jnp.float32), handed_f).astype(jnp.bfloat16)
    added = jnp.einsum('bji,bkjl->bkil', handed_f, carried.astype(jnp.float32))
    return (base.astype(jnp.float32) + added / P_SIZE).astype(jnp.bfloat16)

def reference(wave_first, wave_second, onsite_first, onsite_second, left_first, right_first, left_base, right_second, sources, block_dims):
    live = live_mask(block_dims)
    result_first = lax.map(lambda group: davidson(group[0], group[1], group[2], group[3], live, sources), (wave_first, onsite_first, left_first, right_first))
    handed = jnp.concatenate([jnp.zeros_like(result_first[:1]), result_first[:-1]], axis=0).astype(jnp.bfloat16)
    left_second = lax.map(build_left, (handed, left_base))
    result_second = lax.map(lambda group: davidson(group[0], group[1], group[2], group[3], live, sources), (wave_second, onsite_second, left_second, right_second))
    return (result_first, result_second)
```

```python
import functools

import jax
import jax.numpy as jnp
from jax import lax
from jax.experimental import pallas as pl
from jax.experimental.pallas import tpu as pltpu
from jax.sharding import PartitionSpec as P

STEPS = 3
BLK = 8
TERMS = 16
DIM = 128
QUAD = 4
MESH = pl.DeviceIdType.MESH
F32, BF16 = jnp.float32, jnp.bfloat16


def dot(a, b):
    return jnp.dot(a, b, preferred_element_type=F32)


def folded(x):
    return jnp.sum(x.reshape(DIM // 8, 8, DIM), axis=0)


def kernel(
    nseg, nsec, entries,
    wave0, wave1, onsite0, onsite1, left0, right0, left1, right1, sources, dims,
    out0, out1,
    v, h, hinv, a_own, left, base, right, ext,
    send_v, send_h, send_a, send_hand, send_r,
    land_v, land_h, land_a, land_hand, land_r,
    sums, shift,
    load_sem, out_sem, v_ss, v_rs, h_ss, h_rs, a_ss, a_rs, r_ss, r_rs, hand_ss, hand_rs,
):
    seg, me = lax.axis_index("seg"), lax.axis_index("sec")
    sides = (lax.rem(me + 1, nsec), lax.rem(me + nsec - 1, nsec))
    seg_next, seg_prev = lax.rem(seg + 1, nseg), lax.rem(seg + nseg - 1, nseg)

    def load(i):
        src, dst = (
            (wave0, v.at[0]), (onsite0, h.at[0]), (left0, left), (right0, right.at[0]),
            (wave1, v.at[1]), (onsite1, h.at[1]), (left1, base), (right1, right.at[1]),
        )[i]
        return pltpu.make_async_copy(src, dst, load_sem.at[i])

    def halo(src, land, ss, rs, side):
        return pltpu.make_async_remote_copy(
            src_ref=src, dst_ref=land, send_sem=ss, recv_sem=rs,
            device_id={"sec": sides[side]}, device_id_type=MESH,
        )

    def v_copy(upd, side):
        return halo(send_v.at[upd], land_v.at[upd, side], v_ss.at[upd, side], v_rs.at[upd, side], side)

    def h_copy(upd, side):
        return halo(send_h.at[upd], land_h.at[upd, side], h_ss.at[upd, side], h_rs.at[upd, side], side)

    def a_copy(par, quad, side):
        rows = pl.ds(quad * QUAD, QUAD)
        return halo(send_a.at[rows], land_a.at[par, side, rows], a_ss.at[quad, side], a_rs.at[par, quad, side], side)

    def r_copy(par, d):
        return pltpu.make_async_remote_copy(
            src_ref=send_r, dst_ref=land_r.at[par, d - 1], send_sem=r_ss.at[d - 1], recv_sem=r_rs.at[par, d - 1],
            device_id={"sec": lax.rem(me + d, nsec)}, device_id_type=MESH,
        )

    def hand_copy(quad):
        rows = pl.ds(quad * QUAD, QUAD)
        return pltpu.make_async_remote_copy(
            src_ref=send_hand.at[rows], dst_ref=land_hand.at[rows], send_sem=hand_ss.at[quad], recv_sem=hand_rs.at[quad],
            device_id={"seg": seg_next}, device_id_type=MESH,
        )

    def live(b):
        row = lax.broadcasted_iota(jnp.int32, (DIM, DIM), 0)
        col = lax.broadcasted_iota(jnp.int32, (DIM, DIM), 1)
        limit = dims[b]
        return (row < limit) & (col < limit)

    for i in range(4):
        load(i).start()

    barrier = pltpu.get_barrier_semaphore()
    for d in range(1, nsec):
        pl.semaphore_signal(barrier, inc=1, device_id={"sec": lax.rem(me + d, nsec)}, device_id_type=MESH)
    for other in (seg_next, seg_prev):
        pl.semaphore_signal(barrier, inc=1, device_id={"seg": other}, device_id_type=MESH)
    pl.semaphore_wait(barrier, nsec + 1)

    def start_wave(upd):
        def one(b, _):
            w = jnp.where(live(b), v[upd, b], 0.0)
            v[upd, b] = w
            send_v[upd, b] = w.astype(BF16)
            return 0

        lax.fori_loop(0, BLK, one, 0, unroll=2)

    def start_onsite(upd):
        def one(b, _):
            inverse = 1.0 / (h[upd, b] + 1.0)
            hinv[upd, b] = inverse
            send_h[upd, b] = inverse.astype(BF16)
            return 0

        lax.fori_loop(0, BLK, one, 0, unroll=2)

    load(0).wait()
    start_wave(0)
    for side in range(2):
        v_copy(0, side).start()
    load(1).wait()
    start_onsite(0)
    for side in range(2):
        h_copy(0, side).start()
    for i in range(4, 8):
        load(i).start()
    load(4).wait()
    start_wave(1)
    load(5).wait()
    start_onsite(1)
    shift[...] = jnp.ones_like(shift)
    load(2).wait()
    load(3).wait()

    def build():
        def quad_step(quad, _):
            hand_copy(quad).wait_recv()

            def one(i, _):
                b = quad * QUAD + i
                handed = jnp.where(seg > 0, land_hand[b], jnp.zeros((DIM, DIM), BF16))
                turned = handed.T
                carried = dot(base[b].reshape(TERMS * DIM, DIM), handed).astype(BF16)
                for k in range(0, TERMS, 2):
                    pair = jnp.concatenate([carried[k * DIM : (k + 1) * DIM], carried[(k + 1) * DIM : (k + 2) * DIM]], axis=1)
                    added = dot(turned, pair)
                    for q in range(2):
                        term = added[:, q * DIM : (q + 1) * DIM] * (1.0 / DIM)
                        left[b, k + q] = (base[b, k + q].astype(F32) + term).astype(BF16)
                return 0

            lax.fori_loop(0, QUAD, one, 0, unroll=2)
            return 0

        lax.fori_loop(0, BLK // QUAD, quad_step, 0)

    def begin(upd):
        for side in range(2):
            v_copy(upd, side).wait_recv()

        def one(b, _):
            ext[b] = land_v[upd, 0, b]
            ext[BLK + b] = send_v[upd, b]
            ext[2 * BLK + b] = land_v[upd, 1, b]
            return 0

        lax.fori_loop(0, BLK, one, 0, unroll=2)

    def step(n, _):
        upd, it = n // STEPS, lax.rem(n, STEPS)
        par = lax.rem(n, 2)

        @pl.when(it == 0)
        def _():
            begin(upd)

        @pl.when(n == STEPS)
        def _():
            load(6).wait()
            load(7).wait()
            build()
            for quad in range(BLK // QUAD):
                hand_copy(quad).wait_send()

        sums[...] = jnp.zeros_like(sums)
        first = (me - 1) * BLK
        guess = shift[0:1, 0:1]

        def quad_step(quad, _):
            for i in range(QUAD):
                b = quad * QUAD + i
                parts = [
                    dot(left[b, k], ext[jnp.clip(sources[b, k] - first, 0, 3 * BLK - 1)]).astype(BF16)
                    for k in range(TERMS)
                ]
                terms = dot(jnp.concatenate(parts, axis=1), right[upd, b].reshape(TERMS * DIM, DIM))
                vec, inverse = v[upd, b], hinv[upd, b]
                image = h[upd, b] * vec + jnp.where(live(b), terms, 0.0)
                along = vec * inverse
                part = vec - (image - guess * vec) * inverse
                a_own[b] = part
                send_a[b] = part.astype(BF16)
                sums[0] += folded(vec * image)
                sums[1] += folded(vec * vec)
                sums[2] += folded(part * part)
                sums[3] += folded(part * along)
                sums[4] += folded(along * along)

            @pl.when(it < STEPS - 1)
            def _():
                for side in range(2):
                    a_copy(par, quad, side).start()

            return 0

        lax.fori_loop(0, BLK // QUAD, quad_step, 0)

        row = lax.broadcasted_iota(jnp.int32, (8, DIM), 0)
        packet = jnp.zeros((8, DIM), F32)
        for i in range(5):
            packet = jnp.where(row == i, jnp.sum(sums[i], axis=0, keepdims=True), packet)
        send_r[...] = packet
        for d in range(1, nsec):
            r_copy(par, d).start()

        @pl.when(n == 0)
        def _():
            for side in range(2):
                v_copy(1, side).start()

        @pl.when(n == 1)
        def _():
            for side in range(2):
                h_copy(1, side).start()

        for d in range(1, nsec):
            r_copy(par, d).wait_recv()
        total = packet
        for d in range(1, nsec):
            total = total + land_r[par, d - 1]
        total = jnp.sum(total, axis=1, keepdims=True)
        quotient = total[0:1] / total[1:2]
        delta = quotient - guess
        square = jnp.maximum(total[2:3] + 2.0 * delta * total[3:4] + delta * delta * total[4:5], 0.0)
        scale = 1.0 / jnp.sqrt(square / entries + 1e-06)
        shift[...] = jnp.broadcast_to(quotient, shift.shape)

        def own(b, _):
            vec = scale * (a_own[b] + delta * (v[upd, b] * hinv[upd, b]))
            v[upd, b] = vec
            ext[BLK + b] = vec.astype(BF16)
            send_hand[b] = vec.astype(BF16)
            return 0

        lax.fori_loop(0, BLK, own, 0, unroll=2)

        @pl.when(it < STEPS - 1)
        def _():
            @pl.when(it == 0)
            def _():
                for side in range(2):
                    h_copy(upd, side).wait_recv()

            for quad in range(BLK // QUAD):
                for side in range(2):
                    a_copy(par, quad, side).wait_recv()

            def near(b, _):
                for side in range(2):
                    at = 2 * BLK * side + b
                    along = ext[at].astype(F32) * land_h[upd, side, b].astype(F32)
                    ext[at] = (scale * (land_a[par, side, b].astype(F32) + delta * along)).astype(BF16)
                return 0

            lax.fori_loop(0, BLK, near, 0)
            for quad in range(BLK // QUAD):
                for side in range(2):
                    a_copy(par, quad, side).wait_send()

        @pl.when(n == STEPS - 1)
        def _():
            for quad in range(BLK // QUAD):
                hand_copy(quad).start()
            pltpu.make_async_copy(v.at[0], out0, out_sem.at[0]).start()
            shift[...] = jnp.ones_like(shift)

        for d in range(1, nsec):
            r_copy(par, d).wait_send()
        return 0

    lax.fori_loop(0, 2 * STEPS, step, 0)
    last = pltpu.make_async_copy(v.at[1], out1, out_sem.at[1])
    last.start()
    for upd in range(2):
        for side in range(2):
            v_copy(upd, side).wait_send()
            h_copy(upd, side).wait_send()
    pltpu.make_async_copy(v.at[0], out0, out_sem.at[0]).wait()
    last.wait()


def on_device(nseg, nsec, *args):
    entries = float(nsec * BLK * DIM * DIM)
    anywhere = pl.BlockSpec(memory_space=pl.ANY)
    scalars = pl.BlockSpec(memory_space=pltpu.SMEM)
    waves, envs = (BLK, DIM, DIM), (BLK, TERMS, DIM, DIM)
    dma = pltpu.SemaphoreType.DMA
    big = [a[0] for a in args[:8]]
    outs = pl.pallas_call(
        functools.partial(kernel, nseg, nsec, entries),
        out_shape=[jax.ShapeDtypeStruct(waves, F32)] * 2,
        in_specs=[anywhere] * 8 + [scalars] * 2,
        out_specs=[anywhere] * 2,
        scratch_shapes=[
            pltpu.VMEM((2, *waves), F32),
            pltpu.VMEM((2, *waves), F32),
            pltpu.VMEM((2, *waves), F32),
            pltpu.VMEM(waves, F32),
            pltpu.VMEM(envs, BF16),
            pltpu.VMEM(envs, BF16),
            pltpu.VMEM((2, *envs), BF16),
            pltpu.VMEM((3 * BLK, DIM, DIM), BF16),
            pltpu.VMEM((2, *waves), BF16),
            pltpu.VMEM((2, *waves), BF16),
            pltpu.VMEM(waves, BF16),
            pltpu.VMEM(waves, BF16),
            pltpu.VMEM((8, DIM), F32),
            pltpu.VMEM((2, 2, *waves), BF16),
            pltpu.VMEM((2, 2, *waves), BF16),
            pltpu.VMEM((2, 2, *waves), BF16),
            pltpu.VMEM(waves, BF16),
            pltpu.VMEM((2, nsec - 1, 8, DIM), F32),
            pltpu.VMEM((5, 8, DIM), F32),
            pltpu.VMEM((8, DIM), F32),
            dma((8,)),
            dma((2,)),
            dma((2, 2)),
            dma((2, 2)),
            dma((2, 2)),
            dma((2, 2)),
            dma((BLK // QUAD, 2)),
            dma((2, BLK // QUAD, 2)),
            dma((nsec - 1,)),
            dma((2, nsec - 1)),
            dma((BLK // QUAD,)),
            dma((BLK // QUAD,)),
        ],
        compiler_params=pltpu.CompilerParams(
            collective_id=0, has_side_effects=True, vmem_limit_bytes=52 * 2**20
        ),
        cost_estimate=pl.CostEstimate(
            flops=7 * BLK * TERMS * 4 * DIM**3, bytes_accessed=20 * 2**20, transcendentals=0
        ),
        name="updates",
    )(*big, *args[8:])
    return tuple(o[None] for o in outs)


def solution(mesh):
    wave, env = P("seg", "sec", None, None), P("seg", "sec", None, None, None)
    return jax.shard_map(
        functools.partial(on_device, mesh.shape["seg"], mesh.shape["sec"]),
        mesh=mesh,
        in_specs=(wave, wave, wave, wave, env, env, env, env, P("sec", None), P("sec")),
        out_specs=(wave, wave),
        check_vma=False,
    )
```

```python
import functools

import jax
import jax.numpy as jnp
from jax import lax
from jax.experimental import pallas as pl
from jax.experimental.pallas import tpu as pltpu
from jax.sharding import PartitionSpec as P

STEPS = 3
BLK = 8
TERMS = 16
DIM = 128
QUAD = 4
PAIR = 2
MESH = pl.DeviceIdType.MESH
F32, BF16 = jnp.float32, jnp.bfloat16


def dot(a, b):
    return jnp.dot(a, b, preferred_element_type=F32)


def folded(x):
    return jnp.sum(x.reshape(DIM // 8, 8, DIM), axis=0)


def kernel(
    nseg, nsec, entries,
    wave0, wave1, onsite0, onsite1, left0, right0, left1, right1, sources_in, dims_in,
    out0, out1,
    v, h, hinv, a_own, left, base, right, ext,
    send_v, send_h, send_a, send_b, send_scale, send_r,
    land_v, land_h, land_a, land_hand_a, land_hand_b, land_scale, land_r, near_b,
    sums, shift, sources, dims,
    load_sem, out_sem, v_ss, v_rs, h_ss, h_rs, a_ss, a_rs, r_ss, r_rs, hand_ss, hand_rs,
):
    seg, me = lax.axis_index("seg"), lax.axis_index("sec")
    sides = (lax.rem(me + 1, nsec), lax.rem(me + nsec - 1, nsec))
    seg_next, seg_prev = lax.rem(seg + 1, nseg), lax.rem(seg + nseg - 1, nseg)

    def load(i):
        src, dst = (
            (wave0, v.at[0]), (onsite0, h.at[0]), (left0, left), (right0, right.at[0]),
            (wave1, v.at[1]), (onsite1, h.at[1]), (left1, base), (right1, right.at[1]),
            (dims_in, dims), (sources_in, sources),
        )[i]
        return pltpu.make_async_copy(src, dst, load_sem.at[i])

    def halo(src, land, ss, rs, side):
        return pltpu.make_async_remote_copy(
            src_ref=src, dst_ref=land, send_sem=ss, recv_sem=rs,
            device_id={"sec": sides[side]}, device_id_type=MESH,
        )

    def v_copy(upd, side):
        return halo(send_v.at[upd], land_v.at[upd, side], v_ss.at[upd, side], v_rs.at[upd, side], side)

    def h_copy(upd, side):
        return halo(send_h.at[upd], land_h.at[upd, side], h_ss.at[upd, side], h_rs.at[upd, side], side)

    def a_copy(par, pair, side):
        rows = pl.ds(pair * PAIR, PAIR)
        return halo(send_a.at[rows], land_a.at[par, side, rows], a_ss.at[pair, side], a_rs.at[par, pair, side], side)

    ny = 4 if nsec % 4 == 0 and nsec > 4 else 2
    nx = nsec // ny
    away = sorted(
        ((dx, dy) for dx in range(nx) for dy in range(ny) if (dx, dy) != (0, 0)),
        key=lambda p: -(min(p[0], nx - p[0]) + min(p[1], ny - p[1])),
    )

    def peer(dx, dy):
        return lax.rem(me // ny + dx, nx) * ny + lax.rem(lax.rem(me, ny) + dy, ny)

    def r_copy(par, i):
        return pltpu.make_async_remote_copy(
            src_ref=send_r, dst_ref=land_r.at[par, i], send_sem=r_ss, recv_sem=r_rs.at[par],
            device_id={"sec": peer(*away[i])}, device_id_type=MESH,
        )

    def r_all(par, sem):
        return pltpu.make_async_copy(land_r.at[par], land_r.at[par], sem)

    def hand_copy(i):
        src, dst = ((send_b, land_hand_b), (send_a, land_hand_a), (send_scale, land_scale))[i]
        return pltpu.make_async_remote_copy(
            src_ref=src, dst_ref=dst, send_sem=hand_ss.at[i], recv_sem=hand_rs.at[i],
            device_id={"seg": seg_next}, device_id_type=MESH,
        )

    def live(b):
        row = lax.broadcasted_iota(jnp.int32, (DIM, DIM), 0)
        col = lax.broadcasted_iota(jnp.int32, (DIM, DIM), 1)
        limit = dims[b]
        return (row < limit) & (col < limit)

    for i in (0, 8, 1, 9, 2, 3):
        load(i).start()

    barrier = pltpu.get_barrier_semaphore()
    for d in range(1, nsec):
        pl.semaphore_signal(barrier, inc=1, device_id={"sec": lax.rem(me + d, nsec)}, device_id_type=MESH)
    for other in (seg_next, seg_prev):
        pl.semaphore_signal(barrier, inc=1, device_id={"seg": other}, device_id_type=MESH)
    pl.semaphore_wait(barrier, nsec + 1)

    def start_wave(upd):
        def one(b, _):
            w = jnp.where(live(b), v[upd, b], 0.0)
            v[upd, b] = w
            send_v[upd, b] = w.astype(BF16)
            return 0

        lax.fori_loop(0, BLK, one, 0, unroll=2)

    def start_onsite(upd):
        def one(b, _):
            inverse = 1.0 / (h[upd, b] + 1.0)
            hinv[upd, b] = inverse
            send_h[upd, b] = inverse.astype(BF16)
            return 0

        lax.fori_loop(0, BLK, one, 0, unroll=2)

    load(0).wait()
    load(8).wait()
    start_wave(0)
    for side in range(2):
        v_copy(0, side).start()
    load(1).wait()
    start_onsite(0)
    for i in range(4, 8):
        load(i).start()
    load(4).wait()
    start_wave(1)
    load(5).wait()
    start_onsite(1)
    for side in range(2):
        v_copy(0, side).wait_send()
    for side in range(2):
        h_copy(0, side).start()
    for i in (9, 2, 3):
        load(i).wait()

    def build():
        for i in range(3):
            hand_copy(i).wait_recv()
        scale, delta = land_scale[0:1, 0:1], land_scale[1:2, 0:1]

        def one(b, _):
            moved = scale * (land_hand_a[b].astype(F32) + delta * land_hand_b[b].astype(F32))
            handed = jnp.where(seg > 0, moved, 0.0).astype(BF16)
            turned = handed.T
            carried = dot(base[b].reshape(TERMS * DIM, DIM), handed).astype(BF16)
            for k in range(0, TERMS, 2):
                pair = jnp.concatenate([carried[k * DIM : (k + 1) * DIM], carried[(k + 1) * DIM : (k + 2) * DIM]], axis=1)
                added = dot(turned, pair)
                for q in range(2):
                    term = added[:, q * DIM : (q + 1) * DIM] * (1.0 / DIM)
                    left[b, k + q] = (base[b, k + q].astype(F32) + term).astype(BF16)
            return 0

        lax.fori_loop(0, BLK, one, 0, unroll=4)

    def begin(upd):
        for side in range(2):
            v_copy(upd, side).wait_recv()

        def one(b, _):
            ext[b] = land_v[upd, 0, b]
            ext[BLK + b] = send_v[upd, b]
            ext[2 * BLK + b] = land_v[upd, 1, b]
            return 0

        lax.fori_loop(0, BLK, one, 0, unroll=2)
        shift[...] = jnp.ones_like(shift)

    def step(upd, it, more):
        par = lax.rem(upd * STEPS + it, 2)
        sums[...] = jnp.zeros_like(sums)
        first = (me - 1) * BLK
        guess = shift[0:1, 0:1]

        def quad_step(quad, _):
            for i in range(QUAD):
                b = quad * QUAD + i
                parts = [
                    dot(left[b, k], ext[jnp.clip(sources[b, k] - first, 0, 3 * BLK - 1)]).astype(BF16)
                    for k in range(TERMS)
                ]
                terms = dot(jnp.concatenate(parts, axis=1), right[upd, b].reshape(TERMS * DIM, DIM))
                vec, inverse = v[upd, b], hinv[upd, b]
                image = h[upd, b] * vec + jnp.where(live(b), terms, 0.0)
                along = vec * inverse
                part = vec - (image - guess * vec) * inverse
                a_own[b] = part
                send_a[b] = part.astype(BF16)
                sums[0] += folded(vec * image)
                sums[1] += folded(vec * vec)
                sums[2] += folded(part * part)
                sums[3] += folded(part * along)
                sums[4] += folded(along * along)
                if more and i % PAIR == PAIR - 1:
                    for side in range(2):
                        a_copy(it, quad * (QUAD // PAIR) + i // PAIR, side).start()
            return 0

        lax.fori_loop(0, BLK // QUAD, quad_step, 0)

        row = lax.broadcasted_iota(jnp.int32, (8, DIM), 0)
        packet = jnp.zeros((8, DIM), F32)
        for i in range(5):
            packet = jnp.where(row == i, jnp.sum(sums[i], axis=0, keepdims=True), packet)
        send_r[...] = packet
        for i in range(nsec - 1):
            r_copy(par, i).start()

        if more:

            @pl.when(it == 0)
            def _():
                for side in range(2):
                    h_copy(upd, side).wait_recv()

            def toward(b, _):
                for side in range(2):
                    near_b[side, b] = ext[2 * BLK * side + b].astype(F32) * land_h[upd, side, b].astype(F32)
                return 0

            lax.fori_loop(0, BLK, toward, 0)
        else:

            @pl.when(upd == 0)
            def _():
                hand_copy(1).start()

        r_all(par, r_rs.at[par]).wait()
        total = packet + jnp.sum(land_r[par], axis=0)
        total = jnp.sum(total, axis=1, keepdims=True)
        quotient = total[0:1] / total[1:2]
        delta = quotient - guess
        square = jnp.maximum(total[2:3] + 2.0 * delta * total[3:4] + delta * delta * total[4:5], 0.0)
        scale = 1.0 / jnp.sqrt(square / entries + 1e-06)
        shift[...] = jnp.broadcast_to(quotient, shift.shape)

        if not more:

            @pl.when(upd == 0)
            def _():
                send_scale[...] = jnp.where(row == 0, scale, delta)
                hand_copy(2).start()
                for side in range(2):
                    h_copy(1, side).start()

        def own(b, _):
            vec = scale * (a_own[b] + delta * (v[upd, b] * hinv[upd, b]))
            v[upd, b] = vec
            if more:
                ext[BLK + b] = vec.astype(BF16)
            return 0

        lax.fori_loop(0, BLK, own, 0, unroll=2)

        if more:
            for pair in range(BLK // PAIR):
                for side in range(2):
                    a_copy(it, pair, side).wait_recv()

            def near(b, _):
                for side in range(2):
                    ext[2 * BLK * side + b] = (
                        scale * (land_a[it, side, b].astype(F32) + delta * near_b[side, b])
                    ).astype(BF16)
                return 0

            lax.fori_loop(0, BLK, near, 0, unroll=2)
            for pair in range(BLK // PAIR):
                for side in range(2):
                    a_copy(it, pair, side).wait_send()
        r_all(par, r_ss).wait()

    def update(upd, _):
        begin(upd)

        @pl.when(upd == 1)
        def _():
            load(6).wait()
            load(7).wait()
            build()
            for i in range(3):
                hand_copy(i).wait_send()

        def each(it, _):
            step(upd, it, True)
            return 0

        lax.fori_loop(0, STEPS - 1, each, 0)

        @pl.when(upd == 0)
        def _():
            for side in range(2):
                v_copy(1, side).start()

            def one(b, _):
                send_b[b] = (v[0, b] * hinv[0, b]).astype(BF16)
                return 0

            lax.fori_loop(0, BLK, one, 0)
            hand_copy(0).start()

        step(upd, STEPS - 1, False)

        @pl.when(upd == 0)
        def _():
            pltpu.make_async_copy(v.at[0], out0, out_sem.at[0]).start()

        return 0

    lax.fori_loop(0, 2, update, 0)
    last = pltpu.make_async_copy(v.at[1], out1, out_sem.at[1])
    last.start()
    for side in range(2):
        h_copy(0, side).wait_send()
        v_copy(1, side).wait_send()
        h_copy(1, side).wait_send()
    pltpu.make_async_copy(v.at[0], out0, out_sem.at[0]).wait()
    last.wait()


def on_device(nseg, nsec, *args):
    entries = float(nsec * BLK * DIM * DIM)
    hbm = pl.BlockSpec(memory_space=pltpu.HBM)
    waves, envs = (BLK, DIM, DIM), (BLK, TERMS, DIM, DIM)
    dma = pltpu.SemaphoreType.DMA
    big = [a[0] for a in args[:8]]
    outs = pl.pallas_call(
        functools.partial(kernel, nseg, nsec, entries),
        out_shape=[jax.ShapeDtypeStruct(waves, F32)] * 2,
        in_specs=[hbm] * 10,
        out_specs=[pl.BlockSpec(memory_space=pl.ANY)] * 2,
        scratch_shapes=[
            pltpu.VMEM((2, *waves), F32),
            pltpu.VMEM((2, *waves), F32),
            pltpu.VMEM((2, *waves), F32),
            pltpu.VMEM(waves, F32),
            pltpu.VMEM(envs, BF16),
            pltpu.VMEM(envs, BF16),
            pltpu.VMEM((2, *envs), BF16),
            pltpu.VMEM((3 * BLK, DIM, DIM), BF16),
            pltpu.VMEM((2, *waves), BF16),
            pltpu.VMEM((2, *waves), BF16),
            pltpu.VMEM(waves, BF16),
            pltpu.VMEM(waves, BF16),
            pltpu.VMEM((8, DIM), F32),
            pltpu.VMEM((8, DIM), F32),
            pltpu.VMEM((2, 2, *waves), BF16),
            pltpu.VMEM((2, 2, *waves), BF16),
            pltpu.VMEM((2, 2, *waves), BF16),
            pltpu.VMEM(waves, BF16),
            pltpu.VMEM(waves, BF16),
            pltpu.VMEM((8, DIM), F32),
            pltpu.VMEM((2, nsec - 1, 8, DIM), F32),
            pltpu.VMEM((2, *waves), F32),
            pltpu.VMEM((5, 8, DIM), F32),
            pltpu.VMEM((8, DIM), F32),
            pltpu.SMEM((BLK, TERMS), jnp.int32),
            pltpu.SMEM((BLK,), jnp.int32),
            dma((10,)),
            dma((2,)),
            dma((2, 2)),
            dma((2, 2)),
            dma((2, 2)),
            dma((2, 2)),
            dma((BLK // PAIR, 2)),
            dma((2, BLK // PAIR, 2)),
            dma,
            dma((2,)),
            dma((3,)),
            dma((3,)),
        ],
        compiler_params=pltpu.CompilerParams(
            collective_id=0, has_side_effects=True, vmem_limit_bytes=60 * 2**20
        ),
        cost_estimate=pl.CostEstimate(
            flops=7 * BLK * TERMS * 4 * DIM**3, bytes_accessed=20 * 2**20, transcendentals=0
        ),
        name="updates",
    )(*big, *args[8:])
    return tuple(o[None] for o in outs)


def solution(mesh):
    wave, env = P("seg", "sec", None, None), P("seg", "sec", None, None, None)
    return jax.shard_map(
        functools.partial(on_device, mesh.shape["seg"], mesh.shape["sec"]),
        mesh=mesh,
        in_specs=(wave, wave, wave, wave, env, env, env, env, P("sec", None), P("sec")),
        out_specs=(wave, wave),
        check_vma=False,
    )
```

```python
import functools

import jax
import jax.numpy as jnp
from jax import lax
from jax.experimental import pallas as pl
from jax.experimental.pallas import tpu as pltpu
from jax.sharding import PartitionSpec as P

STEPS = 3
BLK = 8
TERMS = 16
DIM = 128
QUAD = 4
PAIR = 2
MESH = pl.DeviceIdType.MESH
F32, BF16 = jnp.float32, jnp.bfloat16


def dot(a, b):
    return jnp.dot(a, b, preferred_element_type=F32)


def folded(x):
    return jnp.sum(x.reshape(DIM // 8, 8, DIM), axis=0)


def kernel(
    nseg, nsec, entries,
    wave0, wave1, onsite0, onsite1, left0, right0, left1, right1, sources_in, dims_in,
    out0, out1,
    v, h, hinv, a_own, left, base, right, ext,
    send_v, send_h, send_a, send_b, send_scale, send_r,
    land_v, land_h, land_a, land_hand_a, land_hand_b, land_scale, land_r, near_b,
    sums, shift, sources, dims,
    load_sem, out_sem, v_ss, v_rs, h_ss, h_rs, a_ss, a_rs, r_ss, r_rs, hand_ss, hand_rs,
):
    seg, me = lax.axis_index("seg"), lax.axis_index("sec")
    sides = (lax.rem(me + 1, nsec), lax.rem(me + nsec - 1, nsec))
    seg_next, seg_prev = lax.rem(seg + 1, nseg), lax.rem(seg + nseg - 1, nseg)

    def load(i):
        src, dst = (
            (wave0, v.at[0]), (onsite0, h.at[0]), (left0, left), (right0, right.at[0]),
            (wave1, v.at[1]), (onsite1, h.at[1]), (left1, base), (right1, right.at[1]),
            (dims_in, dims), (sources_in, sources),
        )[i]
        return pltpu.make_async_copy(src, dst, load_sem.at[i])

    def halo(src, land, ss, rs, side):
        return pltpu.make_async_remote_copy(
            src_ref=src, dst_ref=land, send_sem=ss, recv_sem=rs,
            device_id={"sec": sides[side]}, device_id_type=MESH,
        )

    def v_copy(upd, side):
        return halo(send_v.at[upd], land_v.at[upd, side], v_ss.at[upd, side], v_rs.at[upd, side], side)

    def h_copy(upd, side):
        return halo(send_h.at[upd], land_h.at[upd, side], h_ss.at[upd, side], h_rs.at[upd, side], side)

    def a_copy(par, pair, side):
        rows = pl.ds(pair * PAIR, PAIR)
        return halo(send_a.at[rows], land_a.at[par, side, rows], a_ss, a_rs.at[par], side)

    def a_all(par, sem):
        return pltpu.make_async_copy(land_a.at[par], land_a.at[par], sem)

    ny = 4 if nsec % 4 == 0 and nsec > 4 else 2
    nx = nsec // ny
    away = sorted(
        ((dx, dy) for dx in range(nx) for dy in range(ny) if (dx, dy) != (0, 0)),
        key=lambda p: -(min(p[0], nx - p[0]) + min(p[1], ny - p[1])),
    )

    peers = [lax.rem(me // ny + dx, nx) * ny + lax.rem(lax.rem(me, ny) + dy, ny) for dx, dy in away]

    def r_copy(par, i):
        return pltpu.make_async_remote_copy(
            src_ref=send_r, dst_ref=land_r.at[par, i], send_sem=r_ss, recv_sem=r_rs.at[par],
            device_id={"sec": peers[i]}, device_id_type=MESH,
        )

    def r_all(par, sem):
        return pltpu.make_async_copy(land_r.at[par], land_r.at[par], sem)

    def hand_copy(i):
        src, dst = ((send_b, land_hand_b), (send_a, land_hand_a), (send_scale, land_scale))[i]
        return pltpu.make_async_remote_copy(
            src_ref=src, dst_ref=dst, send_sem=hand_ss.at[i], recv_sem=hand_rs.at[i],
            device_id={"seg": seg_next}, device_id_type=MESH,
        )

    def result(upd, part):
        rows = pl.ds(part * QUAD, QUAD)
        return pltpu.make_async_copy(v.at[upd, rows], (out0, out1)[upd].at[rows], out_sem.at[upd, part])

    def live(b):
        row = lax.broadcasted_iota(jnp.int32, (DIM, DIM), 0)
        col = lax.broadcasted_iota(jnp.int32, (DIM, DIM), 1)
        limit = dims[b]
        return (row < limit) & (col < limit)

    for i in (0, 8, 1, 9, 2, 3):
        load(i).start()

    barrier = pltpu.get_barrier_semaphore()
    for d in range(1, nsec):
        pl.semaphore_signal(barrier, inc=1, device_id={"sec": lax.rem(me + d, nsec)}, device_id_type=MESH)
    for other in (seg_next, seg_prev):
        pl.semaphore_signal(barrier, inc=1, device_id={"seg": other}, device_id_type=MESH)
    pl.semaphore_wait(barrier, nsec + 1)

    def start_wave(upd):
        def one(b, _):
            w = jnp.where(live(b), v[upd, b], 0.0)
            v[upd, b] = w
            send_v[upd, b] = w.astype(BF16)
            return 0

        lax.fori_loop(0, BLK, one, 0, unroll=2)

    def start_onsite(upd):
        def one(b, _):
            inverse = 1.0 / (h[upd, b] + 1.0)
            hinv[upd, b] = inverse
            send_h[upd, b] = inverse.astype(BF16)
            return 0

        lax.fori_loop(0, BLK, one, 0, unroll=2)

    load(0).wait()
    load(8).wait()
    start_wave(0)
    for side in range(2):
        v_copy(0, side).start()
    load(1).wait()
    start_onsite(0)
    for i in range(4, 8):
        load(i).start()
    load(4).wait()
    start_wave(1)
    load(5).wait()
    start_onsite(1)
    for side in range(2):
        v_copy(0, side).wait_send()
    for side in range(2):
        h_copy(0, side).start()
    for i in (9, 2, 3):
        load(i).wait()

    def build():
        for i in range(3):
            hand_copy(i).wait_recv()
        scale, delta = land_scale[0:1, 0:1], land_scale[1:2, 0:1]

        def one(b, _):
            moved = scale * (land_hand_a[b].astype(F32) + delta * land_hand_b[b].astype(F32))
            handed = jnp.where(seg > 0, moved, 0.0).astype(BF16)
            turned = handed.T
            carried = dot(base[b].reshape(TERMS * DIM, DIM), handed).astype(BF16)
            for k in range(0, TERMS, 2):
                pair = jnp.concatenate([carried[k * DIM : (k + 1) * DIM], carried[(k + 1) * DIM : (k + 2) * DIM]], axis=1)
                added = dot(turned, pair)
                for q in range(2):
                    term = added[:, q * DIM : (q + 1) * DIM] * (1.0 / DIM)
                    left[b, k + q] = (base[b, k + q].astype(F32) + term).astype(BF16)
            return 0

        lax.fori_loop(0, BLK, one, 0, unroll=4)

    def begin(upd):
        for side in range(2):
            v_copy(upd, side).wait_recv()

        def one(b, _):
            ext[b] = land_v[upd, 0, b]
            ext[BLK + b] = send_v[upd, b]
            ext[2 * BLK + b] = land_v[upd, 1, b]
            return 0

        lax.fori_loop(0, BLK, one, 0, unroll=2)
        shift[...] = jnp.ones_like(shift)

    def step(upd, it, more):
        par = lax.rem(upd * STEPS + it, 2)
        sums[...] = jnp.zeros_like(sums)
        first = (me - 1) * BLK
        guess = shift[0:1, 0:1]

        def quad_step(quad, _):
            for i in range(QUAD):
                b = quad * QUAD + i
                parts = [
                    dot(left[b, k], ext[jnp.clip(sources[b, k] - first, 0, 3 * BLK - 1)]).astype(BF16)
                    for k in range(TERMS)
                ]
                terms = dot(jnp.concatenate(parts, axis=1), right[upd, b].reshape(TERMS * DIM, DIM))
                vec, inverse = v[upd, b], hinv[upd, b]
                image = h[upd, b] * vec + jnp.where(live(b), terms, 0.0)
                along = vec * inverse
                part = vec - (image - guess * vec) * inverse
                a_own[b] = part
                send_a[b] = part.astype(BF16)
                sums[0] += folded(vec * image)
                sums[1] += folded(vec * vec)
                sums[2] += folded(part * part)
                sums[3] += folded(part * along)
                sums[4] += folded(along * along)
                if more and i % PAIR == PAIR - 1 and i < QUAD - 1:
                    for side in range(2):
                        a_copy(it, quad * (QUAD // PAIR) + i // PAIR, side).start()
            if more:

                @pl.when(quad == 0)
                def _():
                    for side in range(2):
                        a_copy(it, QUAD // PAIR - 1, side).start()

            return 0

        lax.fori_loop(0, BLK // QUAD, quad_step, 0)

        row = lax.broadcasted_iota(jnp.int32, (8, DIM), 0)
        packet = jnp.zeros((8, DIM), F32)
        for i in range(5):
            packet = jnp.where(row == i, jnp.sum(sums[i], axis=0, keepdims=True), packet)
        send_r[...] = packet
        for i in range(nsec - 1):
            r_copy(par, i).start()

        if more:
            for side in range(2):
                a_copy(it, BLK // PAIR - 1, side).start()

            @pl.when(it == 0)
            def _():
                for side in range(2):
                    h_copy(upd, side).wait_recv()

            def toward(b, _):
                for side in range(2):
                    near_b[side, b] = ext[2 * BLK * side + b].astype(F32) * land_h[upd, side, b].astype(F32)
                return 0

            lax.fori_loop(0, BLK, toward, 0)
        else:

            @pl.when(upd == 0)
            def _():
                hand_copy(1).start()

        r_all(par, r_rs.at[par]).wait()
        total = packet + jnp.sum(land_r[par], axis=0)
        total = jnp.sum(total, axis=1, keepdims=True)
        quotient = total[0:1] / total[1:2]
        delta = quotient - guess
        square = jnp.maximum(total[2:3] + 2.0 * delta * total[3:4] + delta * delta * total[4:5], 0.0)
        scale = 1.0 / jnp.sqrt(square / entries + 1e-06)
        shift[...] = jnp.broadcast_to(quotient, shift.shape)

        if not more:

            @pl.when(upd == 0)
            def _():
                send_scale[...] = jnp.where(row == 0, scale, delta)
                hand_copy(2).start()
                for side in range(2):
                    h_copy(1, side).start()

        def own(b, _):
            vec = scale * (a_own[b] + delta * (v[upd, b] * hinv[upd, b]))
            v[upd, b] = vec
            if more:
                ext[BLK + b] = vec.astype(BF16)
            return 0

        if more:
            lax.fori_loop(0, BLK, own, 0, unroll=4)
        else:
            for part in range(2):
                lax.fori_loop(part * QUAD, (part + 1) * QUAD, own, 0, unroll=4)

                @pl.when(upd == 0)
                def _():
                    result(0, part).start()

                @pl.when(upd == 1)
                def _():
                    result(1, part).start()


        if more:
            a_all(it, a_rs.at[it]).wait()

            def near(b, _):
                for side in range(2):
                    ext[2 * BLK * side + b] = (
                        scale * (land_a[it, side, b].astype(F32) + delta * near_b[side, b])
                    ).astype(BF16)
                return 0

            lax.fori_loop(0, BLK, near, 0, unroll=2)
            a_all(it, a_ss).wait()
        r_all(par, r_ss).wait()

    def update(upd, _):
        begin(upd)

        @pl.when(upd == 1)
        def _():
            load(6).wait()
            load(7).wait()
            build()
            for i in range(3):
                hand_copy(i).wait_send()

        def each(it, _):
            step(upd, it, True)
            return 0

        lax.fori_loop(0, STEPS - 1, each, 0)

        @pl.when(upd == 0)
        def _():
            for side in range(2):
                v_copy(1, side).start()

            def one(b, _):
                send_b[b] = (v[0, b] * hinv[0, b]).astype(BF16)
                return 0

            lax.fori_loop(0, BLK, one, 0)
            hand_copy(0).start()

        step(upd, STEPS - 1, False)

        return 0

    lax.fori_loop(0, 2, update, 0)
    for side in range(2):
        h_copy(0, side).wait_send()
        v_copy(1, side).wait_send()
        h_copy(1, side).wait_send()
    for upd in range(2):
        for part in range(2):
            result(upd, part).wait()


def handed_out(in0, in1, out0, out1, sem, buf):
    ins = [pltpu.make_async_copy(a, buf.at[i], sem.at[i]) for i, a in enumerate((in0, in1))]
    outs = [pltpu.make_async_copy(buf.at[i], a, sem.at[i]) for i, a in enumerate((out0, out1))]
    for copy in ins:
        copy.start()
    for i, o in zip(ins, outs):
        i.wait()
        o.start()
    for copy in outs:
        copy.wait()


def on_device(nseg, nsec, *args):
    entries = float(nsec * BLK * DIM * DIM)
    hbm, anywhere = pl.BlockSpec(memory_space=pltpu.HBM), pl.BlockSpec(memory_space=pl.ANY)
    waves, envs = (BLK, DIM, DIM), (BLK, TERMS, DIM, DIM)
    dma = pltpu.SemaphoreType.DMA
    big = [a[0] for a in args[:8]]
    outs = pl.pallas_call(
        functools.partial(kernel, nseg, nsec, entries),
        out_shape=[jax.ShapeDtypeStruct(waves, F32)] * 2,
        in_specs=[hbm] * 10,
        out_specs=[anywhere] * 2,
        scratch_shapes=[
            pltpu.VMEM((2, *waves), F32),
            pltpu.VMEM((2, *waves), F32),
            pltpu.VMEM((2, *waves), F32),
            pltpu.VMEM(waves, F32),
            pltpu.VMEM(envs, BF16),
            pltpu.VMEM(envs, BF16),
            pltpu.VMEM((2, *envs), BF16),
            pltpu.VMEM((3 * BLK, DIM, DIM), BF16),
            pltpu.VMEM((2, *waves), BF16),
            pltpu.VMEM((2, *waves), BF16),
            pltpu.VMEM(waves, BF16),
            pltpu.VMEM(waves, BF16),
            pltpu.VMEM((8, DIM), F32),
            pltpu.VMEM((8, DIM), F32),
            pltpu.VMEM((2, 2, *waves), BF16),
            pltpu.VMEM((2, 2, *waves), BF16),
            pltpu.VMEM((2, 2, *waves), BF16),
            pltpu.VMEM(waves, BF16),
            pltpu.VMEM(waves, BF16),
            pltpu.VMEM((8, DIM), F32),
            pltpu.VMEM((2, nsec - 1, 8, DIM), F32),
            pltpu.VMEM((2, *waves), F32),
            pltpu.VMEM((5, 8, DIM), F32),
            pltpu.VMEM((8, DIM), F32),
            pltpu.SMEM((BLK, TERMS), jnp.int32),
            pltpu.SMEM((BLK,), jnp.int32),
            dma((10,)),
            dma((2, 2)),
            dma((2, 2)),
            dma((2, 2)),
            dma((2, 2)),
            dma((2, 2)),
            dma,
            dma((2,)),
            dma,
            dma((2,)),
            dma((3,)),
            dma((3,)),
        ],
        compiler_params=pltpu.CompilerParams(
            collective_id=0, has_side_effects=True, vmem_limit_bytes=60 * 2**20
        ),
        cost_estimate=pl.CostEstimate(
            flops=7 * BLK * TERMS * 4 * DIM**3, bytes_accessed=20 * 2**20, transcendentals=0
        ),
        name="updates",
    )(*big, *args[8:])
    outs = pl.pallas_call(
        handed_out,
        out_shape=[jax.ShapeDtypeStruct(waves, F32)] * 2,
        in_specs=[anywhere] * 2,
        out_specs=[hbm] * 2,
        scratch_shapes=[dma((2,)), pltpu.VMEM((2, *waves), F32)],
        name="results",
    )(*outs)
    return tuple(o[None] for o in outs)


def solution(mesh):
    wave, env = P("seg", "sec", None, None), P("seg", "sec", None, None, None)
    return jax.shard_map(
        functools.partial(on_device, mesh.shape["seg"], mesh.shape["sec"]),
        mesh=mesh,
        in_specs=(wave, wave, wave, wave, env, env, env, env, P("sec", None), P("sec")),
        out_specs=(wave, wave),
        check_vma=False,
    )
```

```python
import functools

import jax
import jax.numpy as jnp
from jax import lax
from jax.experimental import pallas as pl
from jax.experimental.pallas import tpu as pltpu
from jax.sharding import PartitionSpec as P

STEPS = 3
BLK = 8
TERMS = 16
DIM = 128
QUAD = 4
PAIR = 2
MESH = pl.DeviceIdType.MESH
F32, BF16 = jnp.float32, jnp.bfloat16


def dot(a, b):
    return jnp.dot(a, b, preferred_element_type=F32)


def folded(x):
    return jnp.sum(x.reshape(DIM // 8, 8, DIM), axis=0)


def kernel(
    nseg, nsec, entries,
    wave0, wave1, onsite0, onsite1, left0, right0, left1, right1, sources_in, dims_in,
    out0, out1,
    v, h, hinv, a_own, left, base, right, ext,
    send_v, send_h, send_a, send_b, send_scale, send_r,
    land_v, land_h, land_a, land_hand_a, land_hand_b, land_scale, land_r, near_b,
    sums, shift, sources, dims,
    load_sem, out_sem, v_ss, v_rs, h_ss, h_rs, a_ss, a_rs, r_ss, r_rs, hand_ss, hand_rs,
):
    seg, me = lax.axis_index("seg"), lax.axis_index("sec")
    sides = (lax.rem(me + 1, nsec), lax.rem(me + nsec - 1, nsec))
    seg_next, seg_prev = lax.rem(seg + 1, nseg), lax.rem(seg + nseg - 1, nseg)

    def load(i):
        src, dst = (
            (wave0, v.at[0]), (onsite0, h.at[0]), (left0, left), (right0, right.at[0]),
            (wave1, v.at[1]), (onsite1, h.at[1]), (left1, base), (right1, right.at[1]),
            (dims_in, dims), (sources_in, sources),
        )[i]
        return pltpu.make_async_copy(src, dst, load_sem.at[i])

    def halo(src, land, ss, rs, side):
        return pltpu.make_async_remote_copy(
            src_ref=src, dst_ref=land, send_sem=ss, recv_sem=rs,
            device_id={"sec": sides[side]}, device_id_type=MESH,
        )

    def v_copy(upd, side):
        return halo(send_v.at[upd], land_v.at[upd, side], v_ss.at[upd, side], v_rs.at[upd, side], side)

    def h_copy(upd, side):
        return halo(send_h.at[upd], land_h.at[upd, side], h_ss.at[upd, side], h_rs.at[upd, side], side)

    def a_copy(par, pair, side):
        rows = pl.ds(pair * PAIR, PAIR)
        return halo(send_a.at[rows], land_a.at[par, side, rows], a_ss, a_rs.at[par], side)

    def a_all(par, sem):
        return pltpu.make_async_copy(land_a.at[par], land_a.at[par], sem)

    ny = 4 if nsec % 4 == 0 and nsec > 4 else 2
    nx = nsec // ny
    away = sorted(
        ((dx, dy) for dx in range(nx) for dy in range(ny) if (dx, dy) != (0, 0)),
        key=lambda p: -(min(p[0], nx - p[0]) + min(p[1], ny - p[1])),
    )

    peers = [lax.rem(me // ny + dx, nx) * ny + lax.rem(lax.rem(me, ny) + dy, ny) for dx, dy in away]

    def r_copy(par, i):
        return pltpu.make_async_remote_copy(
            src_ref=send_r, dst_ref=land_r.at[par, i], send_sem=r_ss, recv_sem=r_rs.at[par],
            device_id={"sec": peers[i]}, device_id_type=MESH,
        )

    def r_all(par, sem):
        return pltpu.make_async_copy(land_r.at[par], land_r.at[par], sem)

    def hand_copy(i):
        src, dst = ((send_b, land_hand_b), (send_a, land_hand_a), (send_scale, land_scale))[i]
        return pltpu.make_async_remote_copy(
            src_ref=src, dst_ref=dst, send_sem=hand_ss.at[i], recv_sem=hand_rs.at[i],
            device_id={"seg": seg_next}, device_id_type=MESH,
        )

    def result(upd, part):
        rows = pl.ds(part * QUAD, QUAD)
        return pltpu.make_async_copy(v.at[upd, rows], (out0, out1)[upd].at[rows], out_sem.at[upd, part])

    def live(b):
        row = lax.broadcasted_iota(jnp.int32, (DIM, DIM), 0)
        col = lax.broadcasted_iota(jnp.int32, (DIM, DIM), 1)
        limit = dims[b]
        return (row < limit) & (col < limit)

    for i in (0, 8, 1, 9, 2, 3):
        load(i).start()

    barrier = pltpu.get_barrier_semaphore()
    for d in range(1, nsec):
        pl.semaphore_signal(barrier, inc=1, device_id={"sec": lax.rem(me + d, nsec)}, device_id_type=MESH)
    for other in (seg_next, seg_prev):
        pl.semaphore_signal(barrier, inc=1, device_id={"seg": other}, device_id_type=MESH)
    pl.semaphore_wait(barrier, nsec + 1)

    def start_wave(upd):
        def one(b, _):
            w = jnp.where(live(b), v[upd, b], 0.0)
            v[upd, b] = w
            send_v[upd, b] = w.astype(BF16)
            return 0

        lax.fori_loop(0, BLK, one, 0, unroll=2)

    def start_onsite(upd):
        def one(b, _):
            inverse = 1.0 / (h[upd, b] + 1.0)
            hinv[upd, b] = inverse
            send_h[upd, b] = inverse.astype(BF16)
            return 0

        lax.fori_loop(0, BLK, one, 0, unroll=2)

    load(0).wait()
    load(8).wait()
    start_wave(0)
    for side in range(2):
        v_copy(0, side).start()
    load(1).wait()
    start_onsite(0)
    for i in range(4, 8):
        load(i).start()
    for side in range(2):
        v_copy(0, side).wait_send()
    for side in range(2):
        h_copy(0, side).start()
    load(4).wait()
    start_wave(1)
    load(5).wait()
    start_onsite(1)
    for i in (9, 2, 3):
        load(i).wait()

    def build():
        for i in range(3):
            hand_copy(i).wait_recv()
        scale, delta = land_scale[0:1, 0:1], land_scale[1:2, 0:1]

        def one(b, _):
            moved = scale * (land_hand_a[b].astype(F32) + delta * land_hand_b[b].astype(F32))
            handed = jnp.where(seg > 0, moved, 0.0).astype(BF16)
            turned = handed.T
            carried = dot(base[b].reshape(TERMS * DIM, DIM), handed).astype(BF16)
            for k in range(0, TERMS, 2):
                pair = jnp.concatenate([carried[k * DIM : (k + 1) * DIM], carried[(k + 1) * DIM : (k + 2) * DIM]], axis=1)
                added = dot(turned, pair)
                for q in range(2):
                    term = added[:, q * DIM : (q + 1) * DIM] * (1.0 / DIM)
                    left[b, k + q] = (base[b, k + q].astype(F32) + term).astype(BF16)
            return 0

        lax.fori_loop(0, BLK, one, 0, unroll=4)

    def begin(upd):
        for side in range(2):
            v_copy(upd, side).wait_recv()

        def one(b, _):
            ext[b] = land_v[upd, 0, b]
            ext[BLK + b] = send_v[upd, b]
            ext[2 * BLK + b] = land_v[upd, 1, b]
            return 0

        lax.fori_loop(0, BLK, one, 0, unroll=2)
        shift[...] = jnp.ones_like(shift)

    def step(upd, it, more):
        par = lax.rem(upd * STEPS + it, 2)
        sums[...] = jnp.zeros_like(sums)
        first = (me - 1) * BLK
        guess = shift[0:1, 0:1]

        def quad_step(quad, _):
            for i in range(QUAD):
                b = quad * QUAD + i
                parts = [
                    dot(left[b, k], ext[jnp.clip(sources[b, k] - first, 0, 3 * BLK - 1)]).astype(BF16)
                    for k in range(TERMS)
                ]
                terms = dot(jnp.concatenate(parts, axis=1), right[upd, b].reshape(TERMS * DIM, DIM))
                vec, inverse = v[upd, b], hinv[upd, b]
                image = h[upd, b] * vec + jnp.where(live(b), terms, 0.0)
                along = vec * inverse
                part = vec - (image - guess * vec) * inverse
                a_own[b] = part
                send_a[b] = part.astype(BF16)
                sums[0] += folded(vec * image)
                sums[1] += folded(vec * vec)
                sums[2] += folded(part * part)
                sums[3] += folded(part * along)
                sums[4] += folded(along * along)
                if more and i % PAIR == PAIR - 1 and i < QUAD - 1:
                    for side in range(2):
                        a_copy(it, quad * (QUAD // PAIR) + i // PAIR, side).start()
            if more:

                @pl.when(quad == 0)
                def _():
                    for side in range(2):
                        a_copy(it, QUAD // PAIR - 1, side).start()

            return 0

        lax.fori_loop(0, BLK // QUAD, quad_step, 0)

        row = lax.broadcasted_iota(jnp.int32, (8, DIM), 0)
        packet = jnp.zeros((8, DIM), F32)
        for i in range(5):
            packet = jnp.where(row == i, jnp.sum(sums[i], axis=0, keepdims=True), packet)
        send_r[...] = packet
        for i in range(nsec - 1):
            r_copy(par, i).start()

        if more:
            for side in range(2):
                a_copy(it, BLK // PAIR - 1, side).start()

            @pl.when(it == 0)
            def _():
                for side in range(2):
                    h_copy(upd, side).wait_recv()

            def toward(b, _):
                for side in range(2):
                    near_b[side, b] = ext[2 * BLK * side + b].astype(F32) * land_h[upd, side, b].astype(F32)
                return 0

            lax.fori_loop(0, BLK, toward, 0)
        else:

            @pl.when(upd == 0)
            def _():
                hand_copy(1).start()
                for side in range(2):
                    v_copy(1, side).start()

        r_all(par, r_rs.at[par]).wait()
        total = packet + jnp.sum(land_r[par], axis=0)
        total = jnp.sum(total, axis=1, keepdims=True)
        quotient = total[0:1] / total[1:2]
        delta = quotient - guess
        square = jnp.maximum(total[2:3] + 2.0 * delta * total[3:4] + delta * delta * total[4:5], 0.0)
        scale = 1.0 / jnp.sqrt(square / entries + 1e-06)
        shift[...] = jnp.broadcast_to(quotient, shift.shape)

        if not more:

            @pl.when(upd == 0)
            def _():
                send_scale[...] = jnp.where(row == 0, scale, delta)
                hand_copy(2).start()
                for side in range(2):
                    h_copy(1, side).start()

        def own(b, _):
            vec = scale * (a_own[b] + delta * (v[upd, b] * hinv[upd, b]))
            v[upd, b] = vec
            if more:
                ext[BLK + b] = vec.astype(BF16)
            return 0

        if more:
            lax.fori_loop(0, BLK, own, 0, unroll=4)
        else:
            for part in range(2):
                lax.fori_loop(part * QUAD, (part + 1) * QUAD, own, 0, unroll=4)

                @pl.when(upd == 0)
                def _():
                    result(0, part).start()

                @pl.when(upd == 1)
                def _():
                    result(1, part).start()


        if more:
            a_all(it, a_rs.at[it]).wait()

            def near(b, _):
                for side in range(2):
                    ext[2 * BLK * side + b] = (
                        scale * (land_a[it, side, b].astype(F32) + delta * near_b[side, b])
                    ).astype(BF16)
                return 0

            lax.fori_loop(0, BLK, near, 0, unroll=2)
            a_all(it, a_ss).wait()
        r_all(par, r_ss).wait()

    def update(upd, _):
        @pl.when(upd == 1)
        def _():
            load(6).wait()
            load(7).wait()
            build()
            for i in range(3):
                hand_copy(i).wait_send()

        begin(upd)

        def each(it, _):
            step(upd, it, True)
            return 0

        lax.fori_loop(0, STEPS - 1, each, 0)

        @pl.when(upd == 0)
        def _():
            def one(b, _):
                send_b[b] = (v[0, b] * hinv[0, b]).astype(BF16)
                return 0

            lax.fori_loop(0, BLK, one, 0)
            hand_copy(0).start()

        step(upd, STEPS - 1, False)

        return 0

    lax.fori_loop(0, 2, update, 0)
    for side in range(2):
        h_copy(0, side).wait_send()
        v_copy(1, side).wait_send()
        h_copy(1, side).wait_send()
    for upd in range(2):
        for part in range(2):
            result(upd, part).wait()


def handed_out(in0, in1, out0, out1, sem, buf):
    ins = [pltpu.make_async_copy(a, buf.at[i], sem.at[i]) for i, a in enumerate((in0, in1))]
    outs = [pltpu.make_async_copy(buf.at[i], a, sem.at[i]) for i, a in enumerate((out0, out1))]
    for copy in ins:
        copy.start()
    for i, o in zip(ins, outs):
        i.wait()
        o.start()
    for copy in outs:
        copy.wait()


def on_device(nseg, nsec, *args):
    entries = float(nsec * BLK * DIM * DIM)
    hbm, anywhere = pl.BlockSpec(memory_space=pltpu.HBM), pl.BlockSpec(memory_space=pl.ANY)
    waves, envs = (BLK, DIM, DIM), (BLK, TERMS, DIM, DIM)
    dma = pltpu.SemaphoreType.DMA
    big = [a[0] for a in args[:8]]
    outs = pl.pallas_call(
        functools.partial(kernel, nseg, nsec, entries),
        out_shape=[jax.ShapeDtypeStruct(waves, F32)] * 2,
        in_specs=[hbm] * 10,
        out_specs=[anywhere] * 2,
        scratch_shapes=[
            pltpu.VMEM((2, *waves), F32),
            pltpu.VMEM((2, *waves), F32),
            pltpu.VMEM((2, *waves), F32),
            pltpu.VMEM(waves, F32),
            pltpu.VMEM(envs, BF16),
            pltpu.VMEM(envs, BF16),
            pltpu.VMEM((2, *envs), BF16),
            pltpu.VMEM((3 * BLK, DIM, DIM), BF16),
            pltpu.VMEM((2, *waves), BF16),
            pltpu.VMEM((2, *waves), BF16),
            pltpu.VMEM(waves, BF16),
            pltpu.VMEM(waves, BF16),
            pltpu.VMEM((8, DIM), F32),
            pltpu.VMEM((8, DIM), F32),
            pltpu.VMEM((2, 2, *waves), BF16),
            pltpu.VMEM((2, 2, *waves), BF16),
            pltpu.VMEM((2, 2, *waves), BF16),
            pltpu.VMEM(waves, BF16),
            pltpu.VMEM(waves, BF16),
            pltpu.VMEM((8, DIM), F32),
            pltpu.VMEM((2, nsec - 1, 8, DIM), F32),
            pltpu.VMEM((2, *waves), F32),
            pltpu.VMEM((5, 8, DIM), F32),
            pltpu.VMEM((8, DIM), F32),
            pltpu.SMEM((BLK, TERMS), jnp.int32),
            pltpu.SMEM((BLK,), jnp.int32),
            dma((10,)),
            dma((2, 2)),
            dma((2, 2)),
            dma((2, 2)),
            dma((2, 2)),
            dma((2, 2)),
            dma,
            dma((2,)),
            dma,
            dma((2,)),
            dma((3,)),
            dma((3,)),
        ],
        compiler_params=pltpu.CompilerParams(
            collective_id=0, has_side_effects=True, vmem_limit_bytes=60 * 2**20
        ),
        cost_estimate=pl.CostEstimate(
            flops=7 * BLK * TERMS * 4 * DIM**3, bytes_accessed=20 * 2**20, transcendentals=0
        ),
        name="updates",
    )(*big, *args[8:])
    outs = pl.pallas_call(
        handed_out,
        out_shape=[jax.ShapeDtypeStruct(waves, F32)] * 2,
        in_specs=[anywhere] * 2,
        out_specs=[hbm] * 2,
        scratch_shapes=[dma((2,)), pltpu.VMEM((2, *waves), F32)],
        name="results",
    )(*outs)
    return tuple(o[None] for o in outs)


def solution(mesh):
    wave, env = P("seg", "sec", None, None), P("seg", "sec", None, None, None)
    return jax.shard_map(
        functools.partial(on_device, mesh.shape["seg"], mesh.shape["sec"]),
        mesh=mesh,
        in_specs=(wave, wave, wave, wave, env, env, env, env, P("sec", None), P("sec")),
        out_specs=(wave, wave),
        check_vma=False,
    )
```

```python
import functools

import jax
import jax.numpy as jnp
from jax import lax
from jax.experimental import pallas as pl
from jax.experimental.pallas import tpu as pltpu
from jax.sharding import PartitionSpec as P

STEPS = 3
BLK = 8
TERMS = 16
DIM = 128
QUAD = 8
PAIR = 2
MESH = pl.DeviceIdType.MESH
F32, BF16 = jnp.float32, jnp.bfloat16


def dot(a, b):
    return jnp.dot(a, b, preferred_element_type=F32)


def folded(x):
    return jnp.sum(x.reshape(DIM // 8, 8, DIM), axis=0)


def kernel(
    nseg, nsec, entries,
    wave0, wave1, onsite0, onsite1, left0, right0, left1, right1, sources_in, dims_in,
    out0, out1,
    v, h, hinv, a_own, left, base, right, ext,
    send_v, send_h, send_a, send_b, send_scale, send_r,
    land_v, land_h, land_a, land_hand_a, land_hand_b, land_scale, land_r, near_b,
    sums, shift, sources, dims,
    load_sem, out_sem, v_ss, v_rs, h_ss, h_rs, a_ss, a_rs, r_ss, r_rs, hand_ss, hand_rs,
):
    seg, me = lax.axis_index("seg"), lax.axis_index("sec")
    sides = (lax.rem(me + 1, nsec), lax.rem(me + nsec - 1, nsec))
    seg_next, seg_prev = lax.rem(seg + 1, nseg), lax.rem(seg + nseg - 1, nseg)

    def load(i):
        src, dst = (
            (wave0, v.at[0]), (onsite0, h.at[0]), (left0, left), (right0, right.at[0]),
            (wave1, v.at[1]), (onsite1, h.at[1]), (left1, base), (right1, right.at[1]),
            (dims_in, dims), (sources_in, sources),
        )[i]
        return pltpu.make_async_copy(src, dst, load_sem.at[i])

    def halo(src, land, ss, rs, side):
        return pltpu.make_async_remote_copy(
            src_ref=src, dst_ref=land, send_sem=ss, recv_sem=rs,
            device_id={"sec": sides[side]}, device_id_type=MESH,
        )

    def v_copy(upd, side):
        return halo(send_v.at[upd], land_v.at[upd, side], v_ss.at[upd, side], v_rs.at[upd, side], side)

    def h_copy(upd, side):
        return halo(send_h.at[upd], land_h.at[upd, side], h_ss.at[upd, side], h_rs.at[upd, side], side)

    def a_copy(par, pair, side):
        rows = pl.ds(pair * PAIR, PAIR)
        return halo(send_a.at[rows], land_a.at[par, side, rows], a_ss, a_rs.at[par], side)

    def a_all(par, sem):
        return pltpu.make_async_copy(land_a.at[par], land_a.at[par], sem)

    ny = 4 if nsec % 4 == 0 and nsec > 4 else 2
    nx = nsec // ny
    away = sorted(
        ((dx, dy) for dx in range(nx) for dy in range(ny) if (dx, dy) != (0, 0)),
        key=lambda p: -(min(p[0], nx - p[0]) + min(p[1], ny - p[1])),
    )

    peers = [lax.rem(me // ny + dx, nx) * ny + lax.rem(lax.rem(me, ny) + dy, ny) for dx, dy in away]

    def r_copy(par, i):
        return pltpu.make_async_remote_copy(
            src_ref=send_r, dst_ref=land_r.at[par, i], send_sem=r_ss, recv_sem=r_rs.at[par],
            device_id={"sec": peers[i]}, device_id_type=MESH,
        )

    def r_all(par, sem):
        return pltpu.make_async_copy(land_r.at[par], land_r.at[par], sem)

    def hand_copy(i):
        src, dst = ((send_b, land_hand_b), (send_a, land_hand_a), (send_scale, land_scale))[i]
        return pltpu.make_async_remote_copy(
            src_ref=src, dst_ref=dst, send_sem=hand_ss.at[i], recv_sem=hand_rs.at[i],
            device_id={"seg": seg_next}, device_id_type=MESH,
        )

    def result(upd, part):
        rows = pl.ds(part * 4, 4)
        return pltpu.make_async_copy(v.at[upd, rows], (out0, out1)[upd].at[rows], out_sem.at[upd, part])

    def live(b):
        row = lax.broadcasted_iota(jnp.int32, (DIM, DIM), 0)
        col = lax.broadcasted_iota(jnp.int32, (DIM, DIM), 1)
        limit = dims[b]
        return (row < limit) & (col < limit)

    for i in (0, 8, 1, 9, 2, 3):
        load(i).start()

    barrier = pltpu.get_barrier_semaphore()
    for d in range(1, nsec):
        pl.semaphore_signal(barrier, inc=1, device_id={"sec": lax.rem(me + d, nsec)}, device_id_type=MESH)
    for other in (seg_next, seg_prev):
        pl.semaphore_signal(barrier, inc=1, device_id={"seg": other}, device_id_type=MESH)
    pl.semaphore_wait(barrier, nsec + 1)

    def start_wave(upd):
        def one(b, _):
            w = jnp.where(live(b), v[upd, b], 0.0)
            v[upd, b] = w
            send_v[upd, b] = w.astype(BF16)
            return 0

        lax.fori_loop(0, BLK, one, 0, unroll=2)

    def start_onsite(upd):
        def one(b, _):
            inverse = 1.0 / (h[upd, b] + 1.0)
            hinv[upd, b] = inverse
            send_h[upd, b] = inverse.astype(BF16)
            return 0

        lax.fori_loop(0, BLK, one, 0, unroll=2)

    load(0).wait()
    load(8).wait()
    start_wave(0)
    for side in range(2):
        v_copy(0, side).start()
    load(1).wait()
    start_onsite(0)
    for i in range(4, 8):
        load(i).start()
    for side in range(2):
        v_copy(0, side).wait_send()
    for side in range(2):
        h_copy(0, side).start()
    load(4).wait()
    start_wave(1)
    load(5).wait()
    start_onsite(1)
    for i in (9, 2, 3):
        load(i).wait()

    def build():
        for i in range(3):
            hand_copy(i).wait_recv()
        scale, delta = land_scale[0:1, 0:1], land_scale[1:2, 0:1]

        def one(b, _):
            moved = scale * (land_hand_a[b].astype(F32) + delta * land_hand_b[b].astype(F32))
            handed = jnp.where(seg > 0, moved, 0.0).astype(BF16)
            turned = handed.T
            carried = dot(base[b].reshape(TERMS * DIM, DIM), handed).astype(BF16)
            for k in range(0, TERMS, 2):
                pair = jnp.concatenate([carried[k * DIM : (k + 1) * DIM], carried[(k + 1) * DIM : (k + 2) * DIM]], axis=1)
                added = dot(turned, pair)
                for q in range(2):
                    term = added[:, q * DIM : (q + 1) * DIM] * (1.0 / DIM)
                    left[b, k + q] = (base[b, k + q].astype(F32) + term).astype(BF16)
            return 0

        lax.fori_loop(0, BLK, one, 0, unroll=4)

    def begin(upd):
        for side in range(2):
            v_copy(upd, side).wait_recv()

        def one(b, _):
            ext[b] = land_v[upd, 0, b]
            ext[BLK + b] = send_v[upd, b]
            ext[2 * BLK + b] = land_v[upd, 1, b]
            return 0

        lax.fori_loop(0, BLK, one, 0, unroll=2)
        shift[...] = jnp.ones_like(shift)

    def step(upd, it, more):
        par = lax.rem(upd * STEPS + it, 2)
        sums[...] = jnp.zeros_like(sums)
        first = (me - 1) * BLK
        guess = shift[0:1, 0:1]

        def quad_step(quad, _):
            for i in range(QUAD):
                b = quad * QUAD + i
                parts = [
                    dot(left[b, k], ext[jnp.clip(sources[b, k] - first, 0, 3 * BLK - 1)]).astype(BF16)
                    for k in range(TERMS)
                ]
                terms = dot(jnp.concatenate(parts, axis=1), right[upd, b].reshape(TERMS * DIM, DIM))
                vec, inverse = v[upd, b], hinv[upd, b]
                image = h[upd, b] * vec + jnp.where(live(b), terms, 0.0)
                along = vec * inverse
                part = vec - (image - guess * vec) * inverse
                a_own[b] = part
                send_a[b] = part.astype(BF16)
                sums[0] += folded(vec * image)
                sums[1] += folded(vec * vec)
                sums[2] += folded(part * part)
                sums[3] += folded(part * along)
                sums[4] += folded(along * along)
                if more and i % PAIR == PAIR - 1 and i < QUAD - 1:
                    for side in range(2):
                        a_copy(it, quad * (QUAD // PAIR) + i // PAIR, side).start()
            return 0

        lax.fori_loop(0, BLK // QUAD, quad_step, 0)

        row = lax.broadcasted_iota(jnp.int32, (8, DIM), 0)
        packet = jnp.zeros((8, DIM), F32)
        for i in range(5):
            packet = jnp.where(row == i, jnp.sum(sums[i], axis=0, keepdims=True), packet)
        send_r[...] = packet
        for i in range(nsec - 1):
            r_copy(par, i).start()

        if more:
            for side in range(2):
                a_copy(it, BLK // PAIR - 1, side).start()

            @pl.when(it == 0)
            def _():
                for side in range(2):
                    h_copy(upd, side).wait_recv()

            def toward(b, _):
                for side in range(2):
                    near_b[side, b] = ext[2 * BLK * side + b].astype(F32) * land_h[upd, side, b].astype(F32)
                return 0

            lax.fori_loop(0, BLK, toward, 0)
        else:

            @pl.when(upd == 0)
            def _():
                hand_copy(1).start()
                for side in range(2):
                    v_copy(1, side).start()

        r_all(par, r_rs.at[par]).wait()
        total = packet + jnp.sum(land_r[par], axis=0)
        total = jnp.sum(total, axis=1, keepdims=True)
        quotient = total[0:1] / total[1:2]
        delta = quotient - guess
        square = jnp.maximum(total[2:3] + 2.0 * delta * total[3:4] + delta * delta * total[4:5], 0.0)
        scale = 1.0 / jnp.sqrt(square / entries + 1e-06)
        shift[...] = jnp.broadcast_to(quotient, shift.shape)

        if not more:

            @pl.when(upd == 0)
            def _():
                send_scale[...] = jnp.where(row == 0, scale, delta)
                hand_copy(2).start()
                for side in range(2):
                    h_copy(1, side).start()

        def own(b, _):
            vec = scale * (a_own[b] + delta * (v[upd, b] * hinv[upd, b]))
            v[upd, b] = vec
            if more:
                ext[BLK + b] = vec.astype(BF16)
            return 0

        if more:
            lax.fori_loop(0, BLK, own, 0, unroll=4)
        else:
            for part in range(2):
                lax.fori_loop(part * 4, (part + 1) * 4, own, 0, unroll=4)

                @pl.when(upd == 0)
                def _():
                    result(0, part).start()

                @pl.when(upd == 1)
                def _():
                    result(1, part).start()


        if more:
            a_all(it, a_rs.at[it]).wait()

            def near(b, _):
                for side in range(2):
                    ext[2 * BLK * side + b] = (
                        scale * (land_a[it, side, b].astype(F32) + delta * near_b[side, b])
                    ).astype(BF16)
                return 0

            lax.fori_loop(0, BLK, near, 0, unroll=2)
            a_all(it, a_ss).wait()
        r_all(par, r_ss).wait()

    def update(upd, _):
        @pl.when(upd == 1)
        def _():
            load(6).wait()
            load(7).wait()
            build()
            for i in range(3):
                hand_copy(i).wait_send()

        begin(upd)

        def each(it, _):
            step(upd, it, True)
            return 0

        lax.fori_loop(0, STEPS - 1, each, 0)

        @pl.when(upd == 0)
        def _():
            def one(b, _):
                send_b[b] = (v[0, b] * hinv[0, b]).astype(BF16)
                return 0

            lax.fori_loop(0, BLK, one, 0)
            hand_copy(0).start()

        step(upd, STEPS - 1, False)

        return 0

    lax.fori_loop(0, 2, update, 0)
    for side in range(2):
        h_copy(0, side).wait_send()
        v_copy(1, side).wait_send()
        h_copy(1, side).wait_send()
    for upd in range(2):
        for part in range(2):
            result(upd, part).wait()


def handed_out(in0, in1, out0, out1, sem, buf):
    def parts(sources, targets):
        return [
            pltpu.make_async_copy(a.at[pl.ds(PAIR * j, PAIR)], b.at[pl.ds(PAIR * j, PAIR)], sem.at[i, j])
            for i, (a, b) in enumerate(zip(sources, targets))
            for j in range(BLK // PAIR)
        ]

    held = (buf.at[0], buf.at[1])
    ins, outs = parts((in0, in1), held), parts(held, (out0, out1))
    for copy in ins:
        copy.start()
    for arriving, leaving in zip(ins, outs):
        arriving.wait()
        leaving.start()
    for copy in outs:
        copy.wait()


def on_device(nseg, nsec, *args):
    entries = float(nsec * BLK * DIM * DIM)
    hbm, anywhere = pl.BlockSpec(memory_space=pltpu.HBM), pl.BlockSpec(memory_space=pl.ANY)
    waves, envs = (BLK, DIM, DIM), (BLK, TERMS, DIM, DIM)
    dma = pltpu.SemaphoreType.DMA
    big = [a[0] for a in args[:8]]
    outs = pl.pallas_call(
        functools.partial(kernel, nseg, nsec, entries),
        out_shape=[jax.ShapeDtypeStruct(waves, F32)] * 2,
        in_specs=[hbm] * 10,
        out_specs=[anywhere] * 2,
        scratch_shapes=[
            pltpu.VMEM((2, *waves), F32),
            pltpu.VMEM((2, *waves), F32),
            pltpu.VMEM((2, *waves), F32),
            pltpu.VMEM(waves, F32),
            pltpu.VMEM(envs, BF16),
            pltpu.VMEM(envs, BF16),
            pltpu.VMEM((2, *envs), BF16),
            pltpu.VMEM((3 * BLK, DIM, DIM), BF16),
            pltpu.VMEM((2, *waves), BF16),
            pltpu.VMEM((2, *waves), BF16),
            pltpu.VMEM(waves, BF16),
            pltpu.VMEM(waves, BF16),
            pltpu.VMEM((8, DIM), F32),
            pltpu.VMEM((8, DIM), F32),
            pltpu.VMEM((2, 2, *waves), BF16),
            pltpu.VMEM((2, 2, *waves), BF16),
            pltpu.VMEM((2, 2, *waves), BF16),
            pltpu.VMEM(waves, BF16),
            pltpu.VMEM(waves, BF16),
            pltpu.VMEM((8, DIM), F32),
            pltpu.VMEM((2, nsec - 1, 8, DIM), F32),
            pltpu.VMEM((2, *waves), F32),
            pltpu.VMEM((5, 8, DIM), F32),
            pltpu.VMEM((8, DIM), F32),
            pltpu.SMEM((BLK, TERMS), jnp.int32),
            pltpu.SMEM((BLK,), jnp.int32),
            dma((10,)),
            dma((2, 2)),
            dma((2, 2)),
            dma((2, 2)),
            dma((2, 2)),
            dma((2, 2)),
            dma,
            dma((2,)),
            dma,
            dma((2,)),
            dma((3,)),
            dma((3,)),
        ],
        compiler_params=pltpu.CompilerParams(
            collective_id=0, has_side_effects=True, vmem_limit_bytes=60 * 2**20
        ),
        cost_estimate=pl.CostEstimate(
            flops=7 * BLK * TERMS * 4 * DIM**3, bytes_accessed=20 * 2**20, transcendentals=0
        ),
        name="updates",
    )(*big, *args[8:])
    outs = pl.pallas_call(
        handed_out,
        out_shape=[jax.ShapeDtypeStruct(waves, F32)] * 2,
        in_specs=[anywhere] * 2,
        out_specs=[hbm] * 2,
        scratch_shapes=[dma((2, BLK // PAIR)), pltpu.VMEM((2, *waves), F32)],
        name="results",
    )(*outs)
    return tuple(o[None] for o in outs)


def solution(mesh):
    wave, env = P("seg", "sec", None, None), P("seg", "sec", None, None, None)
    return jax.shard_map(
        functools.partial(on_device, mesh.shape["seg"], mesh.shape["sec"]),
        mesh=mesh,
        in_specs=(wave, wave, wave, wave, env, env, env, env, P("sec", None), P("sec")),
        out_specs=(wave, wave),
        check_vma=False,
    )
```

```python
import functools

import jax
import jax.numpy as jnp
from jax import lax
from jax.experimental import pallas as pl
from jax.experimental.pallas import tpu as pltpu
from jax.sharding import PartitionSpec as P

STEPS = 3
BLK = 8
TERMS = 16
DIM = 128
QUAD = 8
PAIR = 2
MESH = pl.DeviceIdType.MESH
F32, BF16 = jnp.float32, jnp.bfloat16


def dot(a, b):
    return jnp.dot(a, b, preferred_element_type=F32)


def folded(x):
    return jnp.sum(x.reshape(DIM // 8, 8, DIM), axis=0)


def kernel(
    nseg, nsec, entries,
    wave0, wave1, onsite0, onsite1, left0, right0, left1, right1, sources_in, dims_in,
    out0, out1,
    v, h, hinv, a_own, left, base, right, ext,
    send_v, send_h, send_a, send_b, send_scale, send_r,
    land_v, land_h, land_a, land_hand_a, land_hand_b, land_scale, land_r, near_b,
    sums, shift, sources, dims,
    load_sem, out_sem, v_ss, v_rs, h_ss, h_rs, a_ss, a_rs, r_ss, r_rs, hand_ss, hand_rs,
):
    seg, me = lax.axis_index("seg"), lax.axis_index("sec")
    sides = (lax.rem(me + 1, nsec), lax.rem(me + nsec - 1, nsec))
    seg_next, seg_prev = lax.rem(seg + 1, nseg), lax.rem(seg + nseg - 1, nseg)

    def load(i):
        src, dst = (
            (wave0, v.at[0]), (onsite0, h.at[0]), (left0, left), (right0, right.at[0]),
            (wave1, v.at[1]), (onsite1, h.at[1]), (left1, base), (right1, right.at[1]),
            (dims_in, dims), (sources_in, sources),
        )[i]
        return pltpu.make_async_copy(src, dst, load_sem.at[i])

    def halo(src, land, ss, rs, side):
        return pltpu.make_async_remote_copy(
            src_ref=src, dst_ref=land, send_sem=ss, recv_sem=rs,
            device_id={"sec": sides[side]}, device_id_type=MESH,
        )

    def v_copy(upd, side):
        return halo(send_v.at[upd], land_v.at[upd, side], v_ss.at[upd, side], v_rs.at[upd, side], side)

    def h_copy(upd, side):
        return halo(send_h.at[upd], land_h.at[upd, side], h_ss.at[upd, side], h_rs.at[upd, side], side)

    def a_copy(par, pair, side):
        rows = pl.ds(pair * PAIR, PAIR)
        return halo(send_a.at[rows], land_a.at[par, side, rows], a_ss, a_rs.at[par], side)

    def a_all(par, sem):
        return pltpu.make_async_copy(land_a.at[par], land_a.at[par], sem)

    ny = 4 if nsec % 4 == 0 and nsec > 4 else 2
    nx = nsec // ny
    away = sorted(
        ((dx, dy) for dx in range(nx) for dy in range(ny) if (dx, dy) != (0, 0)),
        key=lambda p: -(min(p[0], nx - p[0]) + min(p[1], ny - p[1])),
    )

    peers = [lax.rem(me // ny + dx, nx) * ny + lax.rem(lax.rem(me, ny) + dy, ny) for dx, dy in away]

    def r_copy(par, i):
        return pltpu.make_async_remote_copy(
            src_ref=send_r, dst_ref=land_r.at[par, i], send_sem=r_ss, recv_sem=r_rs.at[par],
            device_id={"sec": peers[i]}, device_id_type=MESH,
        )

    def r_all(par, sem):
        return pltpu.make_async_copy(land_r.at[par], land_r.at[par], sem)

    def hand_copy(i):
        src, dst = ((send_b, land_hand_b), (send_a, land_hand_a), (send_scale, land_scale))[i]
        return pltpu.make_async_remote_copy(
            src_ref=src, dst_ref=dst, send_sem=hand_ss.at[i], recv_sem=hand_rs.at[i],
            device_id={"seg": seg_next}, device_id_type=MESH,
        )

    def result(upd, part):
        rows = pl.ds(part * 4, 4)
        return pltpu.make_async_copy(v.at[upd, rows], (out0, out1)[upd].at[rows], out_sem.at[upd, part])

    def live(b):
        row = lax.broadcasted_iota(jnp.int32, (DIM, DIM), 0)
        col = lax.broadcasted_iota(jnp.int32, (DIM, DIM), 1)
        limit = dims[b]
        return (row < limit) & (col < limit)

    for i in (0, 8):
        load(i).start()

    barrier = pltpu.get_barrier_semaphore()
    for d in range(1, nsec):
        pl.semaphore_signal(barrier, inc=1, device_id={"sec": lax.rem(me + d, nsec)}, device_id_type=MESH)
    for other in (seg_next, seg_prev):
        pl.semaphore_signal(barrier, inc=1, device_id={"seg": other}, device_id_type=MESH)
    pl.semaphore_wait(barrier, nsec + 1)

    def start_wave(upd):
        def one(b, _):
            w = jnp.where(live(b), v[upd, b], 0.0)
            v[upd, b] = w
            send_v[upd, b] = w.astype(BF16)
            return 0

        lax.fori_loop(0, BLK, one, 0, unroll=2)

    def start_onsite(upd):
        def one(b, _):
            inverse = 1.0 / (h[upd, b] + 1.0)
            hinv[upd, b] = inverse
            send_h[upd, b] = inverse.astype(BF16)
            return 0

        lax.fori_loop(0, BLK, one, 0, unroll=2)

    load(0).wait()
    load(8).wait()
    start_wave(0)
    for side in range(2):
        v_copy(0, side).start()
    for i in (1, 9, 2, 3):
        load(i).start()
    load(1).wait()
    start_onsite(0)
    for i in range(4, 8):
        load(i).start()
    for side in range(2):
        v_copy(0, side).wait_send()
    for side in range(2):
        h_copy(0, side).start()
    load(4).wait()
    start_wave(1)
    load(5).wait()
    start_onsite(1)
    for i in (9, 2, 3):
        load(i).wait()

    def build():
        for i in range(3):
            hand_copy(i).wait_recv()
        scale, delta = land_scale[0:1, 0:1], land_scale[1:2, 0:1]

        def one(b, _):
            moved = scale * (land_hand_a[b].astype(F32) + delta * land_hand_b[b].astype(F32))
            handed = jnp.where(seg > 0, moved, 0.0).astype(BF16)
            turned = handed.T
            carried = dot(base[b].reshape(TERMS * DIM, DIM), handed).astype(BF16)
            for k in range(0, TERMS, 2):
                pair = jnp.concatenate([carried[k * DIM : (k + 1) * DIM], carried[(k + 1) * DIM : (k + 2) * DIM]], axis=1)
                added = dot(turned, pair)
                for q in range(2):
                    term = added[:, q * DIM : (q + 1) * DIM] * (1.0 / DIM)
                    left[b, k + q] = (base[b, k + q].astype(F32) + term).astype(BF16)
            return 0

        lax.fori_loop(0, BLK, one, 0, unroll=4)

    def begin(upd):
        for side in range(2):
            v_copy(upd, side).wait_recv()

        def one(b, _):
            ext[b] = land_v[upd, 0, b]
            ext[BLK + b] = send_v[upd, b]
            ext[2 * BLK + b] = land_v[upd, 1, b]
            return 0

        lax.fori_loop(0, BLK, one, 0, unroll=2)
        shift[...] = jnp.ones_like(shift)

    def step(upd, it, more):
        par = lax.rem(upd * STEPS + it, 2)
        sums[...] = jnp.zeros_like(sums)
        first = (me - 1) * BLK
        guess = shift[0:1, 0:1]

        def quad_step(quad, _):
            for i in range(QUAD):
                b = quad * QUAD + i
                parts = [
                    dot(left[b, k], ext[jnp.clip(sources[b, k] - first, 0, 3 * BLK - 1)]).astype(BF16)
                    for k in range(TERMS)
                ]
                terms = dot(jnp.concatenate(parts, axis=1), right[upd, b].reshape(TERMS * DIM, DIM))
                vec, inverse = v[upd, b], hinv[upd, b]
                image = h[upd, b] * vec + jnp.where(live(b), terms, 0.0)
                along = vec * inverse
                part = vec - (image - guess * vec) * inverse
                a_own[b] = part
                send_a[b] = part.astype(BF16)
                sums[0] += folded(vec * image)
                sums[1] += folded(vec * vec)
                sums[2] += folded(part * part)
                sums[3] += folded(part * along)
                sums[4] += folded(along * along)
                if more and i % PAIR == PAIR - 1 and i < QUAD - 1:
                    for side in range(2):
                        a_copy(it, quad * (QUAD // PAIR) + i // PAIR, side).start()
            return 0

        lax.fori_loop(0, BLK // QUAD, quad_step, 0)

        row = lax.broadcasted_iota(jnp.int32, (8, DIM), 0)
        packet = jnp.zeros((8, DIM), F32)
        for i in range(5):
            packet = jnp.where(row == i, jnp.sum(sums[i], axis=0, keepdims=True), packet)
        send_r[...] = packet
        for i in range(nsec - 1):
            r_copy(par, i).start()

        if more:
            for side in range(2):
                a_copy(it, BLK // PAIR - 1, side).start()

            @pl.when(it == 0)
            def _():
                for side in range(2):
                    h_copy(upd, side).wait_recv()

            def toward(b, _):
                for side in range(2):
                    near_b[side, b] = ext[2 * BLK * side + b].astype(F32) * land_h[upd, side, b].astype(F32)
                return 0

            lax.fori_loop(0, BLK, toward, 0)
        else:

            @pl.when(upd == 0)
            def _():
                hand_copy(1).start()
                for side in range(2):
                    v_copy(1, side).start()

        r_all(par, r_rs.at[par]).wait()
        total = packet + jnp.sum(land_r[par], axis=0)
        total = jnp.sum(total, axis=1, keepdims=True)
        quotient = total[0:1] / total[1:2]
        delta = quotient - guess
        square = jnp.maximum(total[2:3] + 2.0 * delta * total[3:4] + delta * delta * total[4:5], 0.0)
        scale = 1.0 / jnp.sqrt(square / entries + 1e-06)
        shift[...] = jnp.broadcast_to(quotient, shift.shape)

        if not more:

            @pl.when(upd == 0)
            def _():
                send_scale[...] = jnp.where(row == 0, scale, delta)
                hand_copy(2).start()
                for side in range(2):
                    h_copy(1, side).start()

        def own(b, _):
            vec = scale * (a_own[b] + delta * (v[upd, b] * hinv[upd, b]))
            v[upd, b] = vec
            if more:
                ext[BLK + b] = vec.astype(BF16)
            return 0

        if more:
            lax.fori_loop(0, BLK, own, 0, unroll=4)
        else:
            for part in range(2):
                lax.fori_loop(part * 4, (part + 1) * 4, own, 0, unroll=4)

                @pl.when(upd == 0)
                def _():
                    result(0, part).start()

                @pl.when(upd == 1)
                def _():
                    result(1, part).start()


        if more:
            a_all(it, a_rs.at[it]).wait()

            def near(b, _):
                for side in range(2):
                    ext[2 * BLK * side + b] = (
                        scale * (land_a[it, side, b].astype(F32) + delta * near_b[side, b])
                    ).astype(BF16)
                return 0

            lax.fori_loop(0, BLK, near, 0, unroll=2)
            a_all(it, a_ss).wait()
        r_all(par, r_ss).wait()

    def update(upd, _):
        @pl.when(upd == 1)
        def _():
            load(6).wait()
            load(7).wait()
            build()
            for i in range(3):
                hand_copy(i).wait_send()

        begin(upd)

        def each(it, _):
            step(upd, it, True)
            return 0

        lax.fori_loop(0, STEPS - 1, each, 0)

        @pl.when(upd == 0)
        def _():
            def one(b, _):
                send_b[b] = (v[0, b] * hinv[0, b]).astype(BF16)
                return 0

            lax.fori_loop(0, BLK, one, 0)
            hand_copy(0).start()

        step(upd, STEPS - 1, False)

        return 0

    lax.fori_loop(0, 2, update, 0)
    for side in range(2):
        h_copy(0, side).wait_send()
        v_copy(1, side).wait_send()
        h_copy(1, side).wait_send()
    for upd in range(2):
        for part in range(2):
            result(upd, part).wait()


def handed_out(in0, in1, out0, out1, sem, buf):
    def parts(sources, targets):
        return [
            pltpu.make_async_copy(a.at[pl.ds(PAIR * j, PAIR)], b.at[pl.ds(PAIR * j, PAIR)], sem.at[i, j])
            for i, (a, b) in enumerate(zip(sources, targets))
            for j in range(BLK // PAIR)
        ]

    held = (buf.at[0], buf.at[1])
    ins, outs = parts((in0, in1), held), parts(held, (out0, out1))
    for copy in ins:
        copy.start()
    for arriving, leaving in zip(ins, outs):
        arriving.wait()
        leaving.start()
    for copy in outs:
        copy.wait()


def on_device(nseg, nsec, *args):
    entries = float(nsec * BLK * DIM * DIM)
    hbm, anywhere = pl.BlockSpec(memory_space=pltpu.HBM), pl.BlockSpec(memory_space=pl.ANY)
    waves, envs = (BLK, DIM, DIM), (BLK, TERMS, DIM, DIM)
    dma = pltpu.SemaphoreType.DMA
    big = [a[0] for a in args[:8]]
    outs = pl.pallas_call(
        functools.partial(kernel, nseg, nsec, entries),
        out_shape=[jax.ShapeDtypeStruct(waves, F32)] * 2,
        in_specs=[hbm] * 10,
        out_specs=[anywhere] * 2,
        scratch_shapes=[
            pltpu.VMEM((2, *waves), F32),
            pltpu.VMEM((2, *waves), F32),
            pltpu.VMEM((2, *waves), F32),
            pltpu.VMEM(waves, F32),
            pltpu.VMEM(envs, BF16),
            pltpu.VMEM(envs, BF16),
            pltpu.VMEM((2, *envs), BF16),
            pltpu.VMEM((3 * BLK, DIM, DIM), BF16),
            pltpu.VMEM((2, *waves), BF16),
            pltpu.VMEM((2, *waves), BF16),
            pltpu.VMEM(waves, BF16),
            pltpu.VMEM(waves, BF16),
            pltpu.VMEM((8, DIM), F32),
            pltpu.VMEM((8, DIM), F32),
            pltpu.VMEM((2, 2, *waves), BF16),
            pltpu.VMEM((2, 2, *waves), BF16),
            pltpu.VMEM((2, 2, *waves), BF16),
            pltpu.VMEM(waves, BF16),
            pltpu.VMEM(waves, BF16),
            pltpu.VMEM((8, DIM), F32),
            pltpu.VMEM((2, nsec - 1, 8, DIM), F32),
            pltpu.VMEM((2, *waves), F32),
            pltpu.VMEM((5, 8, DIM), F32),
            pltpu.VMEM((8, DIM), F32),
            pltpu.SMEM((BLK, TERMS), jnp.int32),
            pltpu.SMEM((BLK,), jnp.int32),
            dma((10,)),
            dma((2, 2)),
            dma((2, 2)),
            dma((2, 2)),
            dma((2, 2)),
            dma((2, 2)),
            dma,
            dma((2,)),
            dma,
            dma((2,)),
            dma((3,)),
            dma((3,)),
        ],
        compiler_params=pltpu.CompilerParams(
            collective_id=0, has_side_effects=True, vmem_limit_bytes=60 * 2**20
        ),
        cost_estimate=pl.CostEstimate(
            flops=7 * BLK * TERMS * 4 * DIM**3, bytes_accessed=20 * 2**20, transcendentals=0
        ),
        name="updates",
    )(*big, *args[8:])
    outs = pl.pallas_call(
        handed_out,
        out_shape=[jax.ShapeDtypeStruct(waves, F32)] * 2,
        in_specs=[anywhere] * 2,
        out_specs=[hbm] * 2,
        scratch_shapes=[dma((2, BLK // PAIR)), pltpu.VMEM((2, *waves), F32)],
        name="results",
    )(*outs)
    return tuple(o[None] for o in outs)


def solution(mesh):
    wave, env = P("seg", "sec", None, None), P("seg", "sec", None, None, None)
    return jax.shard_map(
        functools.partial(on_device, mesh.shape["seg"], mesh.shape["sec"]),
        mesh=mesh,
        in_specs=(wave, wave, wave, wave, env, env, env, env, P("sec", None), P("sec")),
        out_specs=(wave, wave),
        check_vma=False,
    )
```
